128 devices in a mesh: ty: 8 (over y, x_lo), tx: 16 (over x_hi, z, core).
Axes of the slice: x: 4 (x_hi: 2, x_lo: 2; x = x_hi * 2 + x_lo), y: 4, z: 4, core: 2. Of those that a mesh axis runs over, the one named last changes fastest.
Arguments:
- features: bfloat16 [256, 12, 128, 128], P(('ty', 'tx')), may hold values from -6 to 6
- conv_kernel: float32 [49, 256], P(None, ('ty', 'tx')), may hold values from -0.875 to 0.875
- conv_bias: float32 [256], P(('ty', 'tx')), may hold values from -3 to 3
- neighbour_face: int32 [12, 4], replicated, may hold values from 0 to 11, as said below
- neighbour_side: int32 [12, 4], replicated, may hold values from 0 to 3
- norm_gain: float32 [256], replicated, may hold values from 0.1 to 1.9
- norm_shift: float32 [256], replicated, may hold values from -3 to 3
- expand_weight: bfloat16 [256, 1024], replicated, may hold values from -0.375 to 0.375
- expand_bias: float32 [1024], replicated, may hold values from -3 to 3
- reduce_weight: bfloat16 [1024, 256], replicated, may hold values from -0.1875 to 0.1875
- reduce_bias: float32 [256], replicated, may hold values from -3 to 3
- layer_scale: float32 [256], replicated, may hold values from 0.5 to 1.5
- project_weight: bfloat16 [256, 512], replicated, may hold values from -0.375 to 0.375
- project_bias: float32 [512], replicated, may hold values from -3 to 3
- input_gates: bfloat16 [512, 1536], replicated, may hold values from -0.25 to 0.25
- input_bias: float32 [1536], replicated, may hold values from -3 to 3
- state_gates: bfloat16 [512, 1536], replicated, may hold values from -0.25 to 0.25
- state_bias: float32 [1536], replicated, may hold values from -3 to 3
- hidden_state: float32 [12, 64, 64, 512], P(None, 'ty', 'tx'), may hold values from -6 to 6
Outputs:
- new_state: float32 [12, 64, 64, 512], P(None, 'ty', 'tx')
The draws below stay inside these ranges and needn't reach their ends.
Inputs may be any that keep to these rules, and one draw needn't show every extreme that they name: Faces are stored in a drawn order. Side s of face f borders side neighbour_side[f, s] of face neighbour_face[f, s], which borders side s of face f back; the 12 faces close into the HEALPix sphere, and positions along two bordering sides run the same way.
All inputs are finite; a program needn't handle non-finite values.
Results may differ from the reference program's by a relative error of at most 0.0032.
Values may be sent and summed in bfloat16 or wider, within the bound.
No kernel may reach another device: no remote copies, remote signals or barrier semaphores. Data moves between devices by JAX's collectives and lax.ppermute only.
A program may use at most 128 MiB of HBM per device.

```python
import jax
import jax.numpy as jnp
import numpy as np
from jax import lax

FACES = 12
KERNEL = 7
C8 = 256
HID8 = 1024
C7 = 512
N7 = 64
N8 = 128


NEIGHBOUR_FACE = np.array([[1, 4, 3, 5], [2, 5, 0, 6], [3, 6, 1, 7], [0, 7, 2, 4], [0, 11, 3, 8], [1, 8, 0, 9], [2, 9, 1, 10], [3, 10, 2, 11], [5, 11, 4, 9], [6, 8, 5, 10], [7, 9, 6, 11], [4, 10, 7, 8]], dtype=np.int32)


NEIGHBOUR_SIDE = np.array([[2, 0, 0, 2], [2, 0, 0, 2], [2, 0, 0, 2], [2, 0, 0, 2], [1, 0, 3, 2], [1, 0, 3, 2], [1, 0, 3, 2], [1, 0, 3, 2], [1, 3, 3, 1], [1, 3, 3, 1], [1, 3, 3, 1], [1, 3, 3, 1]], dtype=np.int32)


def face_slots(key):
    return jax.random.permutation(key, FACES).astype(jnp.int32)


def draw_neighbour_face(key, part):
    slots = face_slots(key)
    geometry = jnp.asarray(NEIGHBOUR_FACE)
    return jnp.zeros((FACES, 4), jnp.int32).at[slots].set(slots[geometry])


def draw_neighbour_side(key, part):
    slots = face_slots(key)
    geometry = jnp.asarray(NEIGHBOUR_SIDE)
    return jnp.zeros((FACES, 4), jnp.int32).at[slots].set(geometry)


def block_scale(key, shape, split, least, largest):
    def one(axis_at, shards_of):
        steps = jax.random.uniform(jax.random.fold_in(jax.random.fold_in(key, 6), axis_at), (shards_of,), jnp.float32, least / len(split), largest / len(split))
        return jnp.repeat(jnp.exp(steps), shape[axis_at] // shards_of).reshape((-1,) + (1,) * (len(shape) - axis_at - 1))

    level = one(*split[0])
    for cut in split[1:]:
        level = level * one(*cut)
    return level


def centred(key, dims, scale, bound, pieces=(), kind=jnp.bfloat16):
    result = jax.random.normal(key, dims, jnp.float32) * scale
    if len(pieces) > 0:
        result = block_scale(key, dims, pieces, -0.22, 0.18) * result
    return jnp.clip(result, min=-bound, max=bound).astype(kind)


def setup_inputs(seed: int = 0) -> dict:
    key_list = jax.random.split(jax.random.key(seed), 20)
    features = centred(key_list[0], (C8, FACES, N8, N8), 1.0, 6.0, ((0, 128),))
    conv_kernel = centred(key_list[1], (KERNEL * KERNEL, C8), (KERNEL * KERNEL) ** -0.5, 0.875, ((1, 128),), jnp.float32)
    conv_bias = centred(key_list[2], (C8,), 0.5, 3.0, ((0, 128),), jnp.float32)
    neighbour_face = draw_neighbour_face(jax.random.fold_in(key_list[19], 71), 0)
    neighbour_side = draw_neighbour_side(jax.random.fold_in(key_list[19], 71), 0)
    norm_gain = jnp.clip(1.0 + 0.18 * jax.random.normal(key_list[5], (C8,), jnp.float32), 0.1, 1.9)
    norm_shift = centred(key_list[6], (C8,), 0.5, 3.0, (), jnp.float32)
    expand_weight = centred(key_list[7], (C8, HID8), C8 ** -0.5, 0.375)
    expand_bias = centred(key_list[8], (HID8,), 0.5, 3.0, (), jnp.float32)
    reduce_weight = centred(key_list[9], (HID8, C8), HID8 ** -0.5, 0.1875)
    reduce_bias = centred(key_list[10], (C8,), 0.5, 3.0, (), jnp.float32)
    layer_scale = jnp.clip(jax.random.uniform(key_list[11], (C8,), jnp.float32, 0.5, 1.5), 0.5, 1.5)
    project_weight = centred(key_list[12], (C8, C7), C8 ** -0.5, 0.375)
    project_bias = centred(key_list[13], (C7,), 0.5, 3.0, (), jnp.float32)
    input_gates = centred(key_list[14], (C7, 3 * C7), C7 ** -0.5, 0.25)
    input_bias = centred(key_list[15], (3 * C7,), 0.5, 3.0, (), jnp.float32)
    state_gates = centred(key_list[16], (C7, 3 * C7), C7 ** -0.5, 0.25)
    state_bias = centred(key_list[17], (3 * C7,), 0.5, 3.0, (), jnp.float32)
    hidden_state = centred(key_list[18], (FACES, N7, N7, C7), 1.0, 6.0, ((1, 8), (2, 16)), jnp.float32)
    return {"features": features, "conv_kernel": conv_kernel, "conv_bias": conv_bias, "neighbour_face": neighbour_face, "neighbour_side": neighbour_side, "norm_gain": norm_gain, "norm_shift": norm_shift, "expand_weight": expand_weight, "expand_bias": expand_bias, "reduce_weight": reduce_weight, "reduce_bias": reduce_bias, "layer_scale": layer_scale, "project_weight": project_weight, "project_bias": project_bias, "input_gates": input_gates, "input_bias": input_bias, "state_gates": state_gates, "state_bias": state_bias, "hidden_state": hidden_state}


EPSILON = 1e-06

def side_strips(source, margin):
    extent = source.shape[-1]
    upper = source[:, :, :margin, :]
    lower = jnp.flip(source[:, :, extent - margin:, :], axis=2)
    leftmost = jnp.swapaxes(source[:, :, :, :margin], 2, 3)
    rightmost = jnp.swapaxes(jnp.flip(source[:, :, :, extent - margin:], axis=3), 2, 3)
    return jnp.stack([upper, lower, leftmost, rightmost], axis=2)

def pad_faces(source, neighbour_face, neighbour_side, margin):
    channels, face_count, extent = (source.shape[0], source.shape[1], source.shape[-1])
    strips = side_strips(source, margin).reshape(channels, face_count * 4, margin, extent)
    lookup = (neighbour_face * 4 + neighbour_side).reshape(-1).astype(jnp.int32)
    borders = jnp.take(strips, lookup, axis=1).reshape(channels, face_count, 4, margin, extent)
    band_upper = jnp.flip(borders[:, :, 0], axis=2)
    band_lower = borders[:, :, 1]
    band_left = jnp.flip(jnp.swapaxes(borders[:, :, 2], 2, 3), axis=3)
    band_right = jnp.swapaxes(borders[:, :, 3], 2, 3)
    upper_left = 0.5 * (band_upper[:, :, :, :1] + band_left[:, :, :1, :])
    upper_right = 0.5 * (band_upper[:, :, :, extent - 1:] + band_right[:, :, :1, :])
    lower_left = 0.5 * (band_lower[:, :, :, :1] + band_left[:, :, extent - 1:, :])
    lower_right = 0.5 * (band_lower[:, :, :, extent - 1:] + band_right[:, :, extent - 1:, :])
    top_rows = jnp.concatenate([upper_left, band_upper, upper_right], axis=3)
    middle = jnp.concatenate([band_left, source, band_right], axis=3)
    bottom_rows = jnp.concatenate([lower_left, band_lower, lower_right], axis=3)
    return jnp.concatenate([top_rows, middle, bottom_rows], axis=2)

def depthwise(inputs, kernel_part, bias_part, neighbour_face, neighbour_side):
    margin = KERNEL // 2
    extent = inputs.shape[-1]
    padded = pad_faces(inputs.astype(jnp.float32), neighbour_face, neighbour_side, margin)
    running = jnp.zeros(inputs.shape, jnp.float32)
    for shift_down in range(KERNEL):
        for shift_across in range(KERNEL):
            weight_row = kernel_part[shift_down * KERNEL + shift_across][:, None, None, None]
            running = running + weight_row * padded[:, :, shift_down:shift_down + extent, shift_across:shift_across + extent]
    return (running + bias_part[:, None, None, None]).astype(jnp.bfloat16)

def mix_channels(inputs, norm_gain, norm_shift, expand_weight, expand_bias, reduce_weight, reduce_bias, layer_scale):
    shape_in = inputs.shape
    values = inputs.reshape(shape_in[0], -1).astype(jnp.float32)
    center = lax.optimization_barrier(jnp.mean(values, axis=0))
    spread = lax.optimization_barrier(jnp.mean(jnp.square(values - center), axis=0))
    normed = ((values - center) * lax.rsqrt(spread + EPSILON) * norm_gain[:, None] + norm_shift[:, None]).astype(jnp.bfloat16)
    hidden_units = lax.dot_general(normed, expand_weight, (((0,), (0,)), ((), ())), preferred_element_type=jnp.float32)
    hidden_units = jax.nn.gelu(hidden_units + expand_bias, approximate=False).astype(jnp.bfloat16)
    reduced = lax.dot_general(reduce_weight, hidden_units, (((0,), (1,)), ((), ())), preferred_element_type=jnp.float32)
    return (layer_scale[:, None] * (reduced + reduce_bias[:, None])).astype(jnp.bfloat16).reshape(shape_in)

def pool_sum(features, update):
    merged = features.astype(jnp.float32) + update.astype(jnp.float32)
    shape_in = merged.shape
    quads = merged.reshape(shape_in[:-2] + (shape_in[-2] // 2, 2, shape_in[-1] // 2, 2))
    return lax.optimization_barrier(jnp.mean(quads, axis=(-3, -1))).astype(jnp.bfloat16)

def recurrent(pooled, hidden_state, project_weight, project_bias, input_gates, input_bias, state_gates, state_bias):
    state_width = hidden_state.shape[-1]
    shape_out = hidden_state.shape
    mapped = lax.dot_general(pooled, project_weight, (((0,), (0,)), ((), ())), preferred_element_type=jnp.float32)
    mapped = (mapped + project_bias).astype(jnp.bfloat16).reshape(-1, state_width)
    previous = hidden_state.reshape(-1, state_width)
    from_input = jnp.dot(mapped, input_gates, preferred_element_type=jnp.float32) + input_bias
    from_state = jnp.dot(previous.astype(jnp.bfloat16), state_gates, preferred_element_type=jnp.float32) + state_bias
    update_gate = jax.nn.sigmoid(from_input[:, :state_width] + from_state[:, :state_width])
    reset_gate = jax.nn.sigmoid(from_input[:, state_width:2 * state_width] + from_state[:, state_width:2 * state_width])
    candidate = jnp.tanh(from_input[:, 2 * state_width:] + reset_gate * from_state[:, 2 * state_width:])
    return ((1.0 - update_gate) * candidate + update_gate * previous).reshape(shape_out)

def reference(features, conv_kernel, conv_bias, neighbour_face, neighbour_side, norm_gain, norm_shift, expand_weight, expand_bias, reduce_weight, reduce_bias, layer_scale, project_weight, project_bias, input_gates, input_bias, state_gates, state_bias, hidden_state):
    groups = C8 // 16
    grouped = features.reshape((groups, 16) + features.shape[1:])
    kernels = jnp.moveaxis(conv_kernel.reshape(KERNEL * KERNEL, groups, 16), 1, 0)
    biases = conv_bias.reshape(groups, 16)

    def conv_group(element):
        return depthwise(element[0], element[1], element[2], neighbour_face, neighbour_side)
    conv_out = lax.map(conv_group, (grouped, kernels, biases)).reshape(features.shape)

    def mix_face(face_block):
        return mix_channels(face_block, norm_gain, norm_shift, expand_weight, expand_bias, reduce_weight, reduce_bias, layer_scale)
    update = jnp.moveaxis(lax.map(mix_face, jnp.moveaxis(conv_out, 1, 0)), 0, 1)
    pooled = pool_sum(features, update)

    def step_face(element):
        return recurrent(element[0][:, None], element[1][None], project_weight, project_bias, input_gates, input_bias, state_gates, state_bias)[0]
    return lax.map(step_face, (jnp.moveaxis(pooled, 1, 0), hidden_state))
```

```python
import jax
import jax.numpy as jnp
from jax import lax
from jax.experimental import pallas as pl
from jax.experimental.pallas import tpu as pltpu
from jax.sharding import PartitionSpec as P

KERNEL = 7
FACES = 12
SIDE = 128
EPSILON = 1e-06
PADDED = SIDE + 16
DEPTH = (KERNEL + 1) * SIDE

f32 = jnp.float32
bf16 = jnp.bfloat16


def iota(shape, axis):
    return lax.broadcasted_iota(jnp.int32, shape, axis)


def flip_head(tile):
    row = iota(tile.shape, 0)
    return jnp.where(
        row == 7,
        pltpu.roll(tile, 7, 0),
        jnp.where(row == 6, pltpu.roll(tile, 5, 0), pltpu.roll(tile, 3, 0)),
    )


def flip_tail(tile):
    row = iota(tile.shape, 0)
    return jnp.where(
        row == 0,
        pltpu.roll(tile, 1, 0),
        jnp.where(row == 1, pltpu.roll(tile, 3, 0), pltpu.roll(tile, 5, 0)),
    )


def lane_row(shape, axis):
    n = iota(shape, axis)
    return (n & ~15) + ((n & 7) << 1) + ((n >> 3) & 1)


def send_kernel(
    face_ref,
    side_ref,
    kernel_ref,
    bias_ref,
    x_ref,
    msg_ref,
    yt_ref,
    strip_ref,
    flip_ref,
    lhs_ref,
    rhs_ref,
    pool_ref,
    out_ref,
):
    n = lane_row((SIDE, SIDE), 1)
    i = iota((SIDE, SIDE), 0)
    raw = iota((SIDE, SIDE), 1)
    pair = ((i >> 4) == (raw >> 4)) & (((i >> 1) & 7) == (raw & 7))
    for half in range(2):
        pool_ref[half * SIDE : (half + 1) * SIDE, :] = jnp.where(
            pair & (((raw >> 3) & 1) == half), 0.25, 0.0
        ).astype(bf16)

    for c in range(2):

        def prepare(f, carry, c=c):
            x = x_ref[c, f].astype(f32)
            y = x.T
            yt_ref[c, f, 8 : 8 + SIDE, :] = y
            strip_ref[c, f * 4] = x[:8]
            flip_ref[c, f * 4] = flip_head(x[:8])
            strip_ref[c, f * 4 + 1] = flip_tail(x[SIDE - 8 :])
            flip_ref[c, f * 4 + 1] = x[SIDE - 8 :]
            strip_ref[c, f * 4 + 2] = y[:8]
            flip_ref[c, f * 4 + 2] = flip_head(y[:8])
            strip_ref[c, f * 4 + 3] = flip_tail(y[SIDE - 8 :])
            flip_ref[c, f * 4 + 3] = y[SIDE - 8 :]
            return carry

        lax.fori_loop(0, FACES, prepare, 0)

    row8 = iota((8, SIDE), 0)
    lane8 = iota((8, SIDE), 1)
    at_left = (lane8 == SIDE - 1 - row8) & (row8 < 3)
    at_right = (lane8 == row8) & (row8 < 3)

    for c in range(2):
        def weights(value):
            high = value.astype(bf16)
            return high, (value - high.astype(f32)).astype(bf16)

        offset = i - n + 3
        head = lane_row((8, SIDE), 1)
        band = jnp.where(row8 < 4, 2 - row8 - head, SIDE + 3 + (row8 - 4) - head)
        band = jnp.where((row8 & 3) == 3, -1, band)
        borders = []
        for q in range(KERNEL):
            total = jnp.zeros((SIDE, SIDE), f32)
            border = jnp.zeros((8, SIDE), f32)
            for p in range(KERNEL):
                weight = kernel_ref[p * KERNEL + q, c]
                total = jnp.where(offset == p, weight, total)
                border = jnp.where(band == p, weight, border)
            high, low = weights(total)
            rhs_ref[q * SIDE : (q + 1) * SIDE, :SIDE] = high
            rhs_ref[q * SIDE : (q + 1) * SIDE, SIDE:] = low
            borders.append(border)
        borders.append(jnp.zeros((SIDE - 8 * KERNEL, SIDE), f32))
        high, low = weights(jnp.concatenate(borders, axis=0))
        rhs_ref[KERNEL * SIDE :, :SIDE] = high
        rhs_ref[KERNEL * SIDE :, SIDE:] = low

        def assemble(f, carry, c=c):
            at = [face_ref[f, s] * 4 + side_ref[f, s] for s in range(4)]
            left = strip_ref[c, at[2]]
            right = strip_ref[c, at[3]]
            yt_ref[c, f, :8, :] = flip_ref[c, at[2]]
            yt_ref[c, f, 8 + SIDE :, :] = right
            bands = jnp.where(
                row8 < 4, strip_ref[c, at[0]], pltpu.roll(strip_ref[c, at[1]], 4, 0)
            )
            upper = jnp.where(at_left, left[:, :1], 0.0) + jnp.where(at_right, right[:, :1], 0.0)
            lower = jnp.where(at_left, left[:, SIDE - 1 :], 0.0) + jnp.where(
                at_right, right[:, SIDE - 1 :], 0.0
            )
            upper = jnp.sum(upper, axis=0, keepdims=True)
            lower = jnp.sum(lower, axis=0, keepdims=True)
            corner = 0.5 * (
                jnp.where(lane8 >= SIDE // 2, bands[:, :1], bands[:, SIDE - 1 :])
                + jnp.where(row8 < 4, upper, lower)
            )
            shifted = []
            for q in range(KERNEL):
                s = 3 - q
                if s > 0:
                    shifted.append(pltpu.roll(jnp.where(lane8 >= SIDE - s, corner, bands), s, 1))
                elif s < 0:
                    shifted.append(pltpu.roll(jnp.where(lane8 < -s, corner, bands), SIDE + s, 1))
                else:
                    shifted.append(bands)
            shifted.append(jnp.zeros((SIDE - 8 * KERNEL, SIDE), f32))
            rows = pl.ds(pl.multiple_of(f * SIDE, SIDE), SIDE)
            lhs_ref[rows, KERNEL * SIDE :] = jnp.concatenate(shifted, axis=0).T.astype(bf16)
            for q in range(KERNEL):
                lhs_ref[rows, q * SIDE : (q + 1) * SIDE] = yt_ref[
                    c, f, 5 + q : 5 + q + SIDE, :
                ].astype(bf16)
            return carry

        lax.fori_loop(0, FACES, assemble, 0)

        bias = bias_ref[c]
        for part in range(3):
            product = jnp.dot(
                lhs_ref[part * 512 : (part + 1) * 512, :],
                rhs_ref[...],
                preferred_element_type=f32,
            )
            conv = product[:, :SIDE] + product[:, SIDE:] + bias
            for g in range(4):
                f = part * 4 + g
                for t in range(16):
                    at = g * SIDE + t * 8
                    out_ref[t, f * 8 : (f + 1) * 8, :] = conv[at : at + 8]
        middle = slice(3 * SIDE, 4 * SIDE)
        pooled = jnp.dot(
            lhs_ref[: 6 * SIDE, middle], pool_ref[:SIDE, :], preferred_element_type=f32
        ) + jnp.dot(lhs_ref[6 * SIDE :, middle], pool_ref[SIDE:, :], preferred_element_type=f32)
        for f in range(6):
            for t in range(16):
                at = f * SIDE + t * 8
                out_ref[t, 96 + f * 8 : 96 + (f + 1) * 8, :] = pooled[at : at + 8]

        def pack(t, carry, c=c):
            block = jnp.concatenate(
                [
                    out_ref[t, pl.ds(0, 48, stride=2), :],
                    out_ref[t, pl.ds(1, 48, stride=2), :],
                    out_ref[t, pl.ds(96, 24, stride=2), :] + out_ref[t, pl.ds(97, 24, stride=2), :],
                    jnp.zeros((8, SIDE), f32),
                ],
                axis=0,
            )
            block = block.T.astype(bf16)
            for ty in range(8):
                msg_ref[ty, t, c * 16 : (c + 1) * 16, :] = block[ty * 16 : (ty + 1) * 16]
            return carry

        lax.fori_loop(0, 16, pack, 0)


def send(features, conv_kernel, conv_bias, neighbour_face, neighbour_side):
    smem = pl.BlockSpec(memory_space=pltpu.SMEM)
    vmem = pl.BlockSpec(memory_space=pltpu.VMEM)
    return pl.pallas_call(
        send_kernel,
        out_shape=jax.ShapeDtypeStruct((8, 16, 32, SIDE), bf16),
        in_specs=[smem, smem, smem, smem, vmem],
        out_specs=vmem,
        scratch_shapes=[
            pltpu.VMEM((2, FACES, PADDED, SIDE), f32),
            pltpu.VMEM((2, FACES * 4, 8, SIDE), f32),
            pltpu.VMEM((2, FACES * 4, 8, SIDE), f32),
            pltpu.VMEM((FACES * SIDE, DEPTH), bf16),
            pltpu.VMEM((DEPTH, 2 * SIDE), bf16),
            pltpu.VMEM((2 * SIDE, SIDE), bf16),
            pltpu.VMEM((16, 144, SIDE), f32),
        ],
        compiler_params=pltpu.CompilerParams(vmem_limit_bytes=40 * 1024 * 1024),
    )(neighbour_face, neighbour_side, conv_kernel, conv_bias, features)


def receive_kernel(
    msg_ref,
    gain_ref,
    shift_ref,
    expand_ref,
    expand_bias_ref,
    reduce_ref,
    reduce_bias_ref,
    scale_ref,
    project_ref,
    project_bias_ref,
    input_ref,
    input_bias_ref,
    state_ref,
    state_bias_ref,
    hidden_ref,
    out_ref,
    wide_ref,
    normed_ref,
    pooled_ref,
    units_ref,
):
    wide_ref[...] = msg_ref[...].astype(f32)
    lane = iota((256, SIDE), 1)
    gain = gain_ref[...]
    shift = shift_ref[...]
    for r in range(16):
        di, ci = r // 8, r % 8
        values = wide_ref[pl.ds(r, 256, stride=16), :]
        center = jnp.sum(values, axis=0, keepdims=True) * (1.0 / 256)
        away = values - center
        spread = jnp.sum(away * away, axis=0, keepdims=True) * (1.0 / 256)
        scaled = away * lax.rsqrt(spread + EPSILON)
        cells = jnp.where(lane < 96, scaled, values).T
        normed = (cells[:96] * gain + shift).astype(bf16)
        rows = slice(ci * 48, (ci + 1) * 48)
        normed_ref[di * 2, rows, :] = normed[:48]
        normed_ref[di * 2 + 1, rows, :] = normed[48:]
        pooled_ref[ci * 48 + di * 24 : ci * 48 + (di + 1) * 24, :] = cells[96:120]

    for m in range(3):
        rows = slice(m * 128, (m + 1) * 128)
        for k in range(4):
            lanes = slice(k * 256, (k + 1) * 256)
            total = None
            for s in range(4):
                hidden = (
                    jnp.dot(
                        normed_ref[s, rows, :], expand_ref[:, lanes], preferred_element_type=f32
                    )
                    + expand_bias_ref[:, lanes]
                )
                unit = hidden * (1.0 + lax.erf(hidden * (0.5**0.5)))
                total = unit if total is None else total + unit
            units_ref[rows, lanes] = total.astype(bf16)

    update = (
        jnp.dot(units_ref[...], reduce_ref[...], preferred_element_type=f32) * 0.125
        + reduce_bias_ref[...]
    ) * scale_ref[...]
    pooled_ref[...] = pooled_ref[...] + update
    pooled = jnp.concatenate(
        [
            pooled_ref[ci * 48 + f * 4 : ci * 48 + f * 4 + 4, :]
            for f in range(FACES)
            for ci in range(8)
        ],
        axis=0,
    ).astype(bf16)
    mapped = (
        jnp.dot(pooled, project_ref[...], preferred_element_type=f32) + project_bias_ref[...]
    ).astype(bf16)
    for m in range(3):
        rows = slice(m * 128, (m + 1) * 128)
        previous = hidden_ref[rows, :]
        from_input = (
            jnp.dot(mapped[rows], input_ref[...], preferred_element_type=f32) + input_bias_ref[...]
        )
        from_state = (
            jnp.dot(previous.astype(bf16), state_ref[...], preferred_element_type=f32)
            + state_bias_ref[...]
        )
        update_gate = jax.nn.sigmoid(from_input[:, :512] + from_state[:, :512])
        reset_gate = jax.nn.sigmoid(from_input[:, 512:1024] + from_state[:, 512:1024])
        candidate = jnp.tanh(from_input[:, 1024:] + reset_gate * from_state[:, 1024:])
        out_ref[rows, :] = candidate + update_gate * (previous - candidate)


def receive(message, *rest):
    vmem = pl.BlockSpec(memory_space=pltpu.VMEM)
    return pl.pallas_call(
        receive_kernel,
        out_shape=jax.ShapeDtypeStruct((384, 512), f32),
        in_specs=[vmem] * 15,
        out_specs=vmem,
        scratch_shapes=[
            pltpu.VMEM((4096, SIDE), f32),
            pltpu.VMEM((4, 384, 256), bf16),
            pltpu.VMEM((384, 256), f32),
            pltpu.VMEM((384, 1024), bf16),
        ],
        compiler_params=pltpu.CompilerParams(vmem_limit_bytes=48 * 1024 * 1024),
    )(message, *rest)


def shards(
    features,
    conv_kernel,
    conv_bias,
    neighbour_face,
    neighbour_side,
    norm_gain,
    norm_shift,
    expand_weight,
    expand_bias,
    reduce_weight,
    reduce_bias,
    layer_scale,
    project_weight,
    project_bias,
    input_gates,
    input_bias,
    state_gates,
    state_bias,
    hidden_state,
):
    message = send(features, conv_kernel, conv_bias, neighbour_face, neighbour_side)
    message = message.reshape(128, 32, SIDE)
    arrived = lax.all_to_all(message, ("ty", "tx"), split_axis=0, concat_axis=0, tiled=True)
    row = lambda v: v.reshape(1, -1)
    result = receive(
        arrived.reshape(4096, SIDE),
        row(norm_gain),
        row(norm_shift),
        expand_weight,
        row(expand_bias),
        reduce_weight,
        row(reduce_bias),
        row(layer_scale),
        project_weight,
        row(project_bias),
        input_gates,
        row(input_bias),
        state_gates,
        row(state_bias),
        hidden_state.reshape(384, 512),
    )
    return result.reshape(hidden_state.shape)


def solution(mesh):
    placed = (
        P(("ty", "tx"), None, None, None),
        P(None, ("ty", "tx")),
        P(("ty", "tx")),
        P(),
        P(),
        P(),
        P(),
        P(),
        P(),
        P(),
        P(),
        P(),
        P(),
        P(),
        P(),
        P(),
        P(),
        P(),
        P(None, "ty", "tx", None),
    )
    return jax.shard_map(
        shards, mesh=mesh, in_specs=placed, out_specs=P(None, "ty", "tx", None), check_vma=False
    )
```

```python
import jax
import jax.numpy as jnp
from jax import lax
from jax.experimental import pallas as pl
from jax.experimental.pallas import tpu as pltpu
from jax.sharding import PartitionSpec as P

KERNEL = 7
FACES = 12
SIDE = 128
EPSILON = 1e-06
PADDED = SIDE + 16
DEPTH = (KERNEL + 1) * SIDE

f32 = jnp.float32
bf16 = jnp.bfloat16


def iota(shape, axis):
    return lax.broadcasted_iota(jnp.int32, shape, axis)


def flip_head(tile):
    row = iota(tile.shape, 0)
    return jnp.where(
        row == 7,
        pltpu.roll(tile, 7, 0),
        jnp.where(row == 6, pltpu.roll(tile, 5, 0), pltpu.roll(tile, 3, 0)),
    )


def flip_tail(tile):
    row = iota(tile.shape, 0)
    return jnp.where(
        row == 0,
        pltpu.roll(tile, 1, 0),
        jnp.where(row == 1, pltpu.roll(tile, 3, 0), pltpu.roll(tile, 5, 0)),
    )


def lane_row(shape, axis):
    n = iota(shape, axis)
    return (n & ~15) + ((n & 7) << 1) + ((n >> 3) & 1)


def weights_kernel(kernel_ref, rhs_ref, pool_ref):
    n = lane_row((SIDE, SIDE), 1)
    i = iota((SIDE, SIDE), 0)
    raw = iota((SIDE, SIDE), 1)
    pair = ((i >> 4) == (raw >> 4)) & (((i >> 1) & 7) == (raw & 7))
    for half in range(2):
        pool_ref[half * SIDE : (half + 1) * SIDE, :] = jnp.where(
            pair & (((raw >> 3) & 1) == half), 0.25, 0.0
        ).astype(bf16)

    row8 = iota((8, SIDE), 0)
    for c in range(2):
        def weights(value):
            high = value.astype(bf16)
            return high, (value - high.astype(f32)).astype(bf16)

        offset = i - n + 3
        head = lane_row((8, SIDE), 1)
        band = jnp.where(row8 < 4, 2 - row8 - head, SIDE + 3 + (row8 - 4) - head)
        band = jnp.where((row8 & 3) == 3, -1, band)
        borders = []
        for q in range(KERNEL):
            total = jnp.zeros((SIDE, SIDE), f32)
            border = jnp.zeros((8, SIDE), f32)
            for p in range(KERNEL):
                weight = kernel_ref[c, p * KERNEL + q]
                total = jnp.where(offset == p, weight, total)
                border = jnp.where(band == p, weight, border)
            high, low = weights(total)
            rhs_ref[c, q * SIDE : (q + 1) * SIDE, :SIDE] = high
            rhs_ref[c, q * SIDE : (q + 1) * SIDE, SIDE:] = low
            borders.append(border)
        borders.append(jnp.zeros((SIDE - 8 * KERNEL, SIDE), f32))
        high, low = weights(jnp.concatenate(borders, axis=0))
        rhs_ref[c, KERNEL * SIDE :, :SIDE] = high
        rhs_ref[c, KERNEL * SIDE :, SIDE:] = low


def send_kernel(
    face_ref,
    side_ref,
    bias_ref,
    rhs_ref,
    pool_ref,
    x_ref,
    msg_ref,
    yt_ref,
    strip_ref,
    flip_ref,
    lhs_ref,
    out_ref,
):
    for c in range(2):

        def prepare(f, c=c):
            x = x_ref[c, f]
            y = x.T.astype(f32)
            x = x.astype(f32)
            yt_ref[c, f, 8 : 8 + SIDE, :] = y
            strip_ref[c, f * 4] = x[:8]
            flip_ref[c, f * 4] = flip_head(x[:8])
            strip_ref[c, f * 4 + 1] = flip_tail(x[SIDE - 8 :])
            flip_ref[c, f * 4 + 1] = x[SIDE - 8 :]
            strip_ref[c, f * 4 + 2] = y[:8]
            flip_ref[c, f * 4 + 2] = flip_head(y[:8])
            strip_ref[c, f * 4 + 3] = flip_tail(y[SIDE - 8 :])
            flip_ref[c, f * 4 + 3] = y[SIDE - 8 :]

        for f in range(FACES):
            prepare(f)

    row8 = iota((8, SIDE), 0)
    lane8 = iota((8, SIDE), 1)
    at_left = (lane8 == SIDE - 1 - row8) & (row8 < 3)
    at_right = (lane8 == row8) & (row8 < 3)

    for c in range(2):
        def assemble(f, c=c):
            at = [face_ref[s, f] * 4 + side_ref[s, f] for s in range(4)]
            left = strip_ref[c, at[2]]
            right = strip_ref[c, at[3]]
            yt_ref[c, f, :8, :] = flip_ref[c, at[2]]
            yt_ref[c, f, 8 + SIDE :, :] = right
            bands = jnp.where(
                row8 < 4, strip_ref[c, at[0]], pltpu.roll(strip_ref[c, at[1]], 4, 0)
            )
            upper = jnp.where(at_left, left[:, :1], 0.0) + jnp.where(at_right, right[:, :1], 0.0)
            lower = jnp.where(at_left, left[:, SIDE - 1 :], 0.0) + jnp.where(
                at_right, right[:, SIDE - 1 :], 0.0
            )
            upper = jnp.sum(upper, axis=0, keepdims=True)
            lower = jnp.sum(lower, axis=0, keepdims=True)
            corner = 0.5 * (
                jnp.where(lane8 >= SIDE // 2, bands[:, :1], bands[:, SIDE - 1 :])
                + jnp.where(row8 < 4, upper, lower)
            )
            shifted = []
            for q in range(KERNEL):
                s = 3 - q
                if s > 0:
                    shifted.append(pltpu.roll(jnp.where(lane8 >= SIDE - s, corner, bands), s, 1))
                elif s < 0:
                    shifted.append(pltpu.roll(jnp.where(lane8 < -s, corner, bands), SIDE + s, 1))
                else:
                    shifted.append(bands)
            shifted.append(jnp.zeros((SIDE - 8 * KERNEL, SIDE), f32))
            rows = slice(f * SIDE, (f + 1) * SIDE)
            lhs_ref[rows, KERNEL * SIDE :] = jnp.concatenate(shifted, axis=0).astype(bf16).T
            for q in range(KERNEL):
                lhs_ref[rows, q * SIDE : (q + 1) * SIDE] = yt_ref[
                    c, f, 5 + q : 5 + q + SIDE, :
                ].astype(bf16)

        for f in range(FACES):
            assemble(f)

        bias = bias_ref[c]
        for part in range(3):
            product = jnp.dot(
                lhs_ref[part * 512 : (part + 1) * 512, :],
                rhs_ref[c],
                preferred_element_type=f32,
            )
            conv = product[:, :SIDE] + product[:, SIDE:] + bias
            for g in range(4):
                f = part * 4 + g
                for t in range(16):
                    at = g * SIDE + t * 8
                    out_ref[t, f * 8 : (f + 1) * 8, :] = conv[at : at + 8]
        middle = slice(3 * SIDE, 4 * SIDE)
        pooled = jnp.dot(
            lhs_ref[: 6 * SIDE, middle], pool_ref[:SIDE, :], preferred_element_type=f32
        ) + jnp.dot(lhs_ref[6 * SIDE :, middle], pool_ref[SIDE:, :], preferred_element_type=f32)
        for f in range(6):
            for t in range(16):
                at = f * SIDE + t * 8
                out_ref[t, 96 + f * 8 : 96 + (f + 1) * 8, :] = pooled[at : at + 8]

        def pack(t, c=c):
            block = jnp.concatenate(
                [
                    out_ref[t, pl.ds(0, 48, stride=2), :],
                    out_ref[t, pl.ds(1, 48, stride=2), :],
                    out_ref[t, pl.ds(96, 24, stride=2), :] + out_ref[t, pl.ds(97, 24, stride=2), :],
                    jnp.zeros((8, SIDE), f32),
                ],
                axis=0,
            )
            block = block.astype(bf16).T
            for ty in range(8):
                msg_ref[ty, t, c * 16 : (c + 1) * 16, :] = block[ty * 16 : (ty + 1) * 16]

        for t in range(16):
            pack(t)


def send(features, conv_kernel, conv_bias, neighbour_face, neighbour_side):
    smem = pl.BlockSpec(memory_space=pltpu.SMEM)
    vmem = pl.BlockSpec(memory_space=pltpu.VMEM)
    rhs, pool = pl.pallas_call(
        weights_kernel,
        out_shape=(
            jax.ShapeDtypeStruct((2, DEPTH, 2 * SIDE), bf16),
            jax.ShapeDtypeStruct((2 * SIDE, SIDE), bf16),
        ),
        in_specs=[smem],
        out_specs=(vmem, vmem),
        cost_estimate=pl.CostEstimate(flops=8000000, bytes_accessed=1200000, transcendentals=0),
        compiler_params=pltpu.CompilerParams(vmem_limit_bytes=4 * 1024 * 1024),
    )(conv_kernel.T)
    return pl.pallas_call(
        send_kernel,
        out_shape=jax.ShapeDtypeStruct((8, 16, 32, SIDE), bf16),
        in_specs=[smem, smem, smem, vmem, vmem, vmem],
        out_specs=vmem,
        scratch_shapes=[
            pltpu.VMEM((2, FACES, PADDED, SIDE), f32),
            pltpu.VMEM((2, FACES * 4, 8, SIDE), f32),
            pltpu.VMEM((2, FACES * 4, 8, SIDE), f32),
            pltpu.VMEM((FACES * SIDE, DEPTH), bf16),
            pltpu.VMEM((16, 144, SIDE), f32),
        ],
        cost_estimate=pl.CostEstimate(
            flops=2 * 2 * 1536 * DEPTH * 256, bytes_accessed=4000000, transcendentals=0
        ),
        compiler_params=pltpu.CompilerParams(vmem_limit_bytes=14 * 1024 * 1024),
    )(neighbour_face.T, neighbour_side.T, conv_bias, rhs, pool, features)


def receive_kernel(
    msg_ref,
    gain_ref,
    shift_ref,
    expand_ref,
    expand_bias_ref,
    reduce_ref,
    reduce_bias_ref,
    scale_ref,
    project_ref,
    project_bias_ref,
    input_ref,
    input_bias_ref,
    previous_ref,
    from_state_ref,
    out_ref,
    wide_ref,
    normed_ref,
    pooled_ref,
    units_ref,
):
    wide_ref[...] = msg_ref[...].astype(f32)
    lane = iota((256, SIDE), 1)
    gain = gain_ref[...]
    shift = shift_ref[...]
    for r in range(16):
        di, ci = r // 8, r % 8
        values = wide_ref[pl.ds(r, 256, stride=16), :]
        center = jnp.sum(values, axis=0, keepdims=True) * (1.0 / 256)
        away = values - center
        spread = jnp.sum(away * away, axis=0, keepdims=True) * (1.0 / 256)
        scaled = away * lax.rsqrt(spread + EPSILON)
        cells = jnp.where(lane < 96, scaled, values).T
        normed = (cells[:96] * gain + shift).astype(bf16)
        rows = slice(ci * 48, (ci + 1) * 48)
        normed_ref[di * 2, rows, :] = normed[:48]
        normed_ref[di * 2 + 1, rows, :] = normed[48:]
        pooled_ref[ci * 48 + di * 24 : ci * 48 + (di + 1) * 24, :] = cells[96:120]

    for m in range(3):
        rows = slice(m * 128, (m + 1) * 128)
        for k in range(4):
            lanes = slice(k * 256, (k + 1) * 256)
            total = None
            for s in range(4):
                hidden = (
                    jnp.dot(
                        normed_ref[s, rows, :], expand_ref[:, lanes], preferred_element_type=f32
                    )
                    + expand_bias_ref[:, lanes]
                )
                unit = hidden * (1.0 + lax.erf(hidden * (0.5**0.5)))
                total = unit if total is None else total + unit
            units_ref[rows, lanes] = total.astype(bf16)

    update = (
        jnp.dot(units_ref[...], reduce_ref[...], preferred_element_type=f32) * 0.125
        + reduce_bias_ref[...]
    ) * scale_ref[...]
    pooled = (pooled_ref[...] + update).astype(bf16)
    mapped = (
        jnp.dot(pooled, project_ref[...], preferred_element_type=f32) + project_bias_ref[...]
    ).astype(bf16)
    for m in range(4):
        rows = slice(m * 96, (m + 1) * 96)
        from_input = (
            jnp.dot(mapped[rows], input_ref[...], preferred_element_type=f32) + input_bias_ref[...]
        )
        update_gate = jax.nn.sigmoid(from_input[:, :512] + from_state_ref[rows, :512])
        reset_gate = jax.nn.sigmoid(from_input[:, 512:1024] + from_state_ref[rows, 512:1024])
        candidate = jnp.tanh(from_input[:, 1024:] + reset_gate * from_state_ref[rows, 1024:])
        new = candidate + update_gate * (previous_ref[rows, :] - candidate)
        for ci in range(2):
            for f in range(FACES):
                at = ci * 48 + f * 4
                out_ref[f, m * 2 + ci] = new[at : at + 4]


def state_kernel(hidden_ref, state_ref, bias_ref, previous_ref, from_state_ref):
    for ci in range(8):
        for f in range(FACES):
            at = ci * 48 + f * 4
            previous_ref[at : at + 4, :] = hidden_ref[f, ci]
    for m in range(3):
        rows = slice(m * 128, (m + 1) * 128)
        from_state_ref[rows, :] = (
            jnp.dot(
                previous_ref[rows, :].astype(bf16), state_ref[...], preferred_element_type=f32
            )
            + bias_ref[...]
        )


def state_part(hidden, state_gates, state_bias):
    vmem = pl.BlockSpec(memory_space=pltpu.VMEM)
    return pl.pallas_call(
        state_kernel,
        out_shape=(
            jax.ShapeDtypeStruct((384, 512), f32),
            jax.ShapeDtypeStruct((384, 1536), f32),
        ),
        in_specs=[vmem] * 3,
        out_specs=(vmem, vmem),
        cost_estimate=pl.CostEstimate(
            flops=2 * 384 * 512 * 1536, bytes_accessed=6000000, transcendentals=0
        ),
        compiler_params=pltpu.CompilerParams(vmem_limit_bytes=10 * 1024 * 1024),
    )(hidden, state_gates, state_bias)


def receive(message, *rest):
    vmem = pl.BlockSpec(memory_space=pltpu.VMEM)
    return pl.pallas_call(
        receive_kernel,
        out_shape=jax.ShapeDtypeStruct((FACES, 8, 4, 512), f32),
        in_specs=[vmem] * 14,
        out_specs=vmem,
        scratch_shapes=[
            pltpu.VMEM((4096, SIDE), f32),
            pltpu.VMEM((4, 384, 256), bf16),
            pltpu.VMEM((384, 256), f32),
            pltpu.VMEM((384, 1024), bf16),
        ],
        cost_estimate=pl.CostEstimate(
            flops=2 * 700000000, bytes_accessed=8000000, transcendentals=2000000
        ),
        compiler_params=pltpu.CompilerParams(vmem_limit_bytes=20 * 1024 * 1024),
    )(message, *rest)


def shards(
    features,
    conv_kernel,
    conv_bias,
    neighbour_face,
    neighbour_side,
    norm_gain,
    norm_shift,
    expand_weight,
    expand_bias,
    reduce_weight,
    reduce_bias,
    layer_scale,
    project_weight,
    project_bias,
    input_gates,
    input_bias,
    state_gates,
    state_bias,
    hidden_state,
):
    message = send(features, conv_kernel, conv_bias, neighbour_face, neighbour_side)
    message = message.reshape(128, 32, SIDE)
    arrived = lax.all_to_all(message, ("ty", "tx"), split_axis=0, concat_axis=0, tiled=True)
    row = lambda v: v.reshape(1, -1)
    previous, from_state = state_part(hidden_state, state_gates, row(state_bias))
    return receive(
        arrived.reshape(4096, SIDE),
        row(norm_gain),
        row(norm_shift),
        expand_weight,
        row(expand_bias),
        reduce_weight,
        row(reduce_bias),
        row(layer_scale),
        project_weight,
        row(project_bias),
        input_gates,
        row(input_bias),
        previous,
        from_state,
    )


def solution(mesh):
    placed = (
        P(("ty", "tx"), None, None, None),
        P(None, ("ty", "tx")),
        P(("ty", "tx")),
        P(),
        P(),
        P(),
        P(),
        P(),
        P(),
        P(),
        P(),
        P(),
        P(),
        P(),
        P(),
        P(),
        P(),
        P(),
        P(None, "ty", "tx", None),
    )
    return jax.shard_map(
        shards, mesh=mesh, in_specs=placed, out_specs=P(None, "ty", "tx", None), check_vma=False
    )
```

```python
import jax
import jax.numpy as jnp
from jax import lax
from jax.experimental import pallas as pl
from jax.experimental.pallas import tpu as pltpu
from jax.sharding import PartitionSpec as P

KERNEL = 7
FACES = 12
SIDE = 128
EPSILON = 1e-06
PADDED = SIDE + 16
DEPTH = (KERNEL + 1) * SIDE

SEND_VMEM = 63 * 1024 * 1024

f32 = jnp.float32
bf16 = jnp.bfloat16


def iota(shape, axis):
    return lax.broadcasted_iota(jnp.int32, shape, axis)


def flip_head(tile):
    row = iota(tile.shape, 0)
    return jnp.where(
        row == 7,
        pltpu.roll(tile, 7, 0),
        jnp.where(row == 6, pltpu.roll(tile, 5, 0), pltpu.roll(tile, 3, 0)),
    )


def flip_tail(tile):
    row = iota(tile.shape, 0)
    return jnp.where(
        row == 0,
        pltpu.roll(tile, 1, 0),
        jnp.where(row == 1, pltpu.roll(tile, 3, 0), pltpu.roll(tile, 5, 0)),
    )


def lane_row(shape, axis):
    n = iota(shape, axis)
    return (n & ~15) + ((n & 7) << 1) + ((n >> 3) & 1)


def send_kernel(
    kernel_hbm,
    face_hbm,
    side_hbm,
    bias_hbm,
    x_hbm,
    msg_hbm,
    kernel_ref,
    face_ref,
    side_ref,
    bias_ref,
    x_ref,
    yt_ref,
    strip_ref,
    flip_ref,
    lhs_ref,
    rhs_ref,
    pool_ref,
    out_ref,
    msg_ref,
    small_sem,
    x_sem,
    msg_sem,
):
    loads = [
        pltpu.make_async_copy(source, target, small_sem.at[k])
        for k, (source, target) in enumerate(
            [
                (kernel_hbm, kernel_ref),
                (face_hbm, face_ref),
                (side_hbm, side_ref),
                (bias_hbm, bias_ref),
            ]
        )
    ] + [pltpu.make_async_copy(x_hbm.at[c], x_ref.at[c], x_sem.at[c]) for c in range(2)]
    for copy in loads:
        copy.start()

    i = iota((SIDE, SIDE), 0)
    raw = iota((SIDE, SIDE), 1)
    pair = ((i >> 4) == (raw >> 4)) & (((i >> 1) & 7) == (raw & 7))
    for half in range(2):
        pool_ref[half * SIDE : (half + 1) * SIDE, :] = jnp.where(
            pair & (((raw >> 3) & 1) == half), 0.25, 0.0
        ).astype(bf16)

    row8 = iota((8, SIDE), 0)
    lane8 = iota((8, SIDE), 1)
    at_left = (lane8 == SIDE - 1 - row8) & (row8 < 3)
    at_right = (lane8 == row8) & (row8 < 3)
    lane16 = iota((16, SIDE), 1)
    offset = 64 + iota((16, SIDE), 0) - lane_row((16, SIDE), 1) + 3
    head = lane_row((8, SIDE), 1)
    band = jnp.where(row8 < 4, 2 - row8 - head, SIDE + 3 + (row8 - 4) - head)
    band = jnp.where((row8 & 3) == 3, -1, band)

    for copy in loads:
        copy.wait()

    def store_weights(c, rows, value):
        high = value.astype(bf16)
        rhs_ref[c, rows, :SIDE] = high
        rhs_ref[c, rows, SIDE:] = (value - high.astype(f32)).astype(bf16)

    for c in range(2):
        borders = []
        for q in range(KERNEL):
            base = jnp.zeros((16, SIDE), f32)
            border = jnp.zeros((8, SIDE), f32)
            for p in range(KERNEL):
                weight = kernel_ref[c, p * KERNEL + q]
                base = jnp.where(offset == p, weight, base)
                border = jnp.where(band == p, weight, border)
            for k in range(8):
                value = base if k == 4 else pltpu.roll(base, (16 * (k - 4)) % SIDE, 1)
                if k == 0:
                    value = jnp.where(lane16 >= SIDE - 16, 0.0, value)
                if k == 7:
                    value = jnp.where(lane16 < 16, 0.0, value)
                at = q * SIDE + k * 16
                store_weights(c, slice(at, at + 16), value)
            borders.append(border)
        borders.append(jnp.zeros((SIDE - 8 * KERNEL, SIDE), f32))
        store_weights(c, slice(KERNEL * SIDE, DEPTH), jnp.concatenate(borders, axis=0))

    for c in range(2):

        def prepare(f, c=c):
            x = x_ref[c, f]
            y = x.T.astype(f32)
            x = x.astype(f32)
            yt_ref[c, f, 8 : 8 + SIDE, :] = y
            strip_ref[c, f * 4] = x[:8]
            flip_ref[c, f * 4] = flip_head(x[:8])
            strip_ref[c, f * 4 + 1] = flip_tail(x[SIDE - 8 :])
            flip_ref[c, f * 4 + 1] = x[SIDE - 8 :]
            strip_ref[c, f * 4 + 2] = y[:8]
            flip_ref[c, f * 4 + 2] = flip_head(y[:8])
            strip_ref[c, f * 4 + 3] = flip_tail(y[SIDE - 8 :])
            flip_ref[c, f * 4 + 3] = y[SIDE - 8 :]

        for f in range(FACES):
            prepare(f)

    sends = []
    for c in range(2):

        def assemble(f, c=c):
            at = [face_ref[s, f] * 4 + side_ref[s, f] for s in range(4)]
            left = strip_ref[c, at[2]]
            right = strip_ref[c, at[3]]
            yt_ref[c, f, :8, :] = flip_ref[c, at[2]]
            yt_ref[c, f, 8 + SIDE :, :] = right
            bands = jnp.where(
                row8 < 4, strip_ref[c, at[0]], pltpu.roll(strip_ref[c, at[1]], 4, 0)
            )
            upper = jnp.where(at_left, left[:, :1], 0.0) + jnp.where(at_right, right[:, :1], 0.0)
            lower = jnp.where(at_left, left[:, SIDE - 1 :], 0.0) + jnp.where(
                at_right, right[:, SIDE - 1 :], 0.0
            )
            upper = jnp.sum(upper, axis=0, keepdims=True)
            lower = jnp.sum(lower, axis=0, keepdims=True)
            corner = 0.5 * (
                jnp.where(lane8 >= SIDE // 2, bands[:, :1], bands[:, SIDE - 1 :])
                + jnp.where(row8 < 4, upper, lower)
            )
            shifted = []
            for q in range(KERNEL):
                s = 3 - q
                if s > 0:
                    shifted.append(pltpu.roll(jnp.where(lane8 >= SIDE - s, corner, bands), s, 1))
                elif s < 0:
                    shifted.append(pltpu.roll(jnp.where(lane8 < -s, corner, bands), SIDE + s, 1))
                else:
                    shifted.append(bands)
            shifted.append(jnp.zeros((SIDE - 8 * KERNEL, SIDE), f32))
            rows = slice(f * SIDE, (f + 1) * SIDE)
            lhs_ref[rows, KERNEL * SIDE :] = jnp.concatenate(shifted, axis=0).astype(bf16).T
            for q in range(KERNEL):
                lhs_ref[rows, q * SIDE : (q + 1) * SIDE] = yt_ref[
                    c, f, 5 + q : 5 + q + SIDE, :
                ].astype(bf16)

        for f in range(FACES):
            assemble(f)

        bias = bias_ref[c]
        for part in range(3):
            product = jnp.dot(
                lhs_ref[part * 512 : (part + 1) * 512, :],
                rhs_ref[c],
                preferred_element_type=f32,
            )
            conv = product[:, :SIDE] + product[:, SIDE:] + bias
            for g in range(4):
                f = part * 4 + g
                for t in range(16):
                    at = g * SIDE + t * 8
                    out_ref[t, f * 8 : (f + 1) * 8, :] = conv[at : at + 8]
        middle = slice(3 * SIDE, 4 * SIDE)
        pooled = jnp.dot(
            lhs_ref[: 6 * SIDE, middle], pool_ref[:SIDE, :], preferred_element_type=f32
        ) + jnp.dot(lhs_ref[6 * SIDE :, middle], pool_ref[SIDE:, :], preferred_element_type=f32)
        for f in range(6):
            for t in range(16):
                at = f * SIDE + t * 8
                out_ref[t, 96 + f * 8 : 96 + (f + 1) * 8, :] = pooled[at : at + 8]

        def pack(t, c=c):
            block = jnp.concatenate(
                [
                    out_ref[t, pl.ds(0, 48, stride=2), :],
                    out_ref[t, pl.ds(1, 48, stride=2), :],
                    out_ref[t, pl.ds(96, 24, stride=2), :] + out_ref[t, pl.ds(97, 24, stride=2), :],
                    jnp.zeros((8, SIDE), f32),
                ],
                axis=0,
            )
            block = block.astype(bf16).T
            for ty in range(8):
                msg_ref[ty, t, c * 16 : (c + 1) * 16, :] = block[ty * 16 : (ty + 1) * 16]

        for t in range(16):
            pack(t)
        sends.append(
            pltpu.make_async_copy(
                msg_ref.at[:, :, pl.ds(c * 16, 16)],
                msg_hbm.at[:, :, pl.ds(c * 16, 16)],
                msg_sem.at[c],
            )
        )
        sends[-1].start()
    for copy in sends:
        copy.wait()


def send(features, conv_kernel, conv_bias, neighbour_face, neighbour_side):
    hbm = pl.BlockSpec(memory_space=pl.ANY)
    return pl.pallas_call(
        send_kernel,
        out_shape=jax.ShapeDtypeStruct((8, 16, 32, SIDE), bf16),
        in_specs=[hbm] * 5,
        out_specs=hbm,
        scratch_shapes=[
            pltpu.SMEM((2, KERNEL * KERNEL), f32),
            pltpu.SMEM((4, FACES), jnp.int32),
            pltpu.SMEM((4, FACES), jnp.int32),
            pltpu.SMEM((2,), f32),
            pltpu.VMEM((2, FACES, SIDE, SIDE), bf16),
            pltpu.VMEM((2, FACES, PADDED, SIDE), f32),
            pltpu.VMEM((2, FACES * 4, 8, SIDE), f32),
            pltpu.VMEM((2, FACES * 4, 8, SIDE), f32),
            pltpu.VMEM((FACES * SIDE, DEPTH), bf16),
            pltpu.VMEM((2, DEPTH, 2 * SIDE), bf16),
            pltpu.VMEM((2 * SIDE, SIDE), bf16),
            pltpu.VMEM((16, 144, SIDE), f32),
            pltpu.VMEM((8, 16, 32, SIDE), bf16),
            pltpu.SemaphoreType.DMA((4,)),
            pltpu.SemaphoreType.DMA((2,)),
            pltpu.SemaphoreType.DMA((2,)),
        ],
        cost_estimate=pl.CostEstimate(
            flops=2 * 2 * 1536 * DEPTH * 256, bytes_accessed=4000000, transcendentals=0
        ),
        compiler_params=pltpu.CompilerParams(vmem_limit_bytes=SEND_VMEM),
    )(conv_kernel.T, neighbour_face.T, neighbour_side.T, conv_bias, features)


def receive_kernel(
    msg_ref,
    gain_ref,
    shift_ref,
    expand_ref,
    expand_bias_ref,
    reduce_ref,
    reduce_bias_ref,
    scale_ref,
    project_ref,
    project_bias_ref,
    input_ref,
    input_bias_ref,
    previous_ref,
    from_state_ref,
    out_ref,
    wide_ref,
    normed_ref,
    pooled_ref,
    units_ref,
):
    wide_ref[...] = msg_ref[...].astype(f32)
    lane = iota((256, SIDE), 1)
    gain = gain_ref[...]
    shift = shift_ref[...]
    for r in range(16):
        di, ci = r // 8, r % 8
        values = wide_ref[pl.ds(r, 256, stride=16), :]
        center = jnp.sum(values, axis=0, keepdims=True) * (1.0 / 256)
        away = values - center
        spread = jnp.sum(away * away, axis=0, keepdims=True) * (1.0 / 256)
        normed = away * lax.rsqrt(spread + EPSILON) * gain + shift
        cells = jnp.where(lane < 96, normed, values).astype(bf16).T
        rows = slice(ci * 48, (ci + 1) * 48)
        normed_ref[di * 2, rows, :] = cells[:48]
        normed_ref[di * 2 + 1, rows, :] = cells[48:96]
        pooled_ref[ci * 48 + di * 24 : ci * 48 + (di + 1) * 24, :] = cells[96:].astype(f32)[:24]

    for k in range(4):
        lanes = slice(k * 256, (k + 1) * 256)
        for m in range(3):
            rows = slice(m * 128, (m + 1) * 128)
            hidden = jnp.dot(
                normed_ref[:, rows, :].reshape(512, 256),
                expand_ref[:, lanes],
                preferred_element_type=f32,
            )
            total = None
            for s in range(4):
                part = hidden[s * 128 : (s + 1) * 128] + expand_bias_ref[:, lanes]
                unit = part * (1.0 + lax.erf(part * (0.5**0.5)))
                total = unit if total is None else total + unit
            units_ref[rows, lanes] = total.astype(bf16)

    update = (
        jnp.dot(units_ref[...], reduce_ref[...], preferred_element_type=f32) * 0.125
        + reduce_bias_ref[...]
    ) * scale_ref[...]
    pooled = (pooled_ref[...] + update).astype(bf16)
    mapped = (
        jnp.dot(pooled, project_ref[...], preferred_element_type=f32) + project_bias_ref[...]
    ).astype(bf16)

    def sigmoid(v):
        return 0.5 * jnp.tanh(0.5 * v) + 0.5

    for k in range(2):

        def gate(block):
            lanes = slice(block * 512 + k * 256, block * 512 + (k + 1) * 256)
            return (
                jnp.dot(mapped, input_ref[:, lanes], preferred_element_type=f32)
                + input_bias_ref[:, lanes],
                from_state_ref[:, lanes],
            )

        lanes = slice(k * 256, (k + 1) * 256)
        a, b = gate(0)
        update_gate = sigmoid(a + b)
        a, b = gate(1)
        reset_gate = sigmoid(a + b)
        a, b = gate(2)
        candidate = jnp.tanh(a + reset_gate * b)
        new = candidate + update_gate * (previous_ref[:, lanes] - candidate)
        for ci in range(8):
            for f in range(FACES):
                at = ci * 48 + f * 4
                out_ref[f, ci, :, lanes] = new[at : at + 4]


def ready_kernel(*refs):
    hidden_ref, state_ref, state_bias_ref, gain_ref, shift_ref = refs[:5]
    vectors, matrices = refs[5:10], refs[10:14]
    previous_ref, from_state_ref, gain_out, shift_out = refs[14:18]
    vectors_out, matrices_out = refs[18:23], refs[23:27]
    sems = refs[27]
    copies = [
        pltpu.make_async_copy(source, target, sems.at[k])
        for k, (source, target) in enumerate(zip(matrices, matrices_out))
    ]
    for copy in copies:
        copy.start()
    for ci in range(8):
        for f in range(FACES):
            at = ci * 48 + f * 4
            previous_ref[at : at + 4, :] = hidden_ref[f, ci]
    for k in range(6):
        lanes = slice(k * 256, (k + 1) * 256)
        from_state_ref[:, lanes] = (
            jnp.dot(
                previous_ref[...].astype(bf16), state_ref[:, lanes], preferred_element_type=f32
            )
            + state_bias_ref[:, lanes]
        )
    for source, target in ((gain_ref, gain_out), (shift_ref, shift_out)):
        for half in range(2):
            row = source[:, half * SIDE : (half + 1) * SIDE]
            target[half * SIDE : (half + 1) * SIDE, :] = jnp.broadcast_to(row, (SIDE, SIDE)).T
    for source, target in zip(vectors, vectors_out):
        target[...] = source[...]
    for copy in copies:
        copy.wait()


def ready(hidden, state_gates, state_bias, gain, shift, vectors, matrices):
    vmem = pl.BlockSpec(memory_space=pltpu.VMEM)
    hbm = pl.BlockSpec(memory_space=pl.ANY)
    shape = lambda v: jax.ShapeDtypeStruct(v.shape, v.dtype)
    outs = [
        jax.ShapeDtypeStruct((384, 512), f32),
        jax.ShapeDtypeStruct((384, 1536), f32),
        jax.ShapeDtypeStruct((256, SIDE), f32),
        jax.ShapeDtypeStruct((256, SIDE), f32),
        *map(shape, vectors),
        *map(shape, matrices),
    ]
    return pl.pallas_call(
        ready_kernel,
        out_shape=outs,
        in_specs=[vmem] * 10 + [hbm] * 4,
        out_specs=[vmem] * len(outs),
        scratch_shapes=[pltpu.SemaphoreType.DMA((4,))],
        cost_estimate=pl.CostEstimate(
            flops=2 * 384 * 512 * 1536, bytes_accessed=12000000, transcendentals=0
        ),
        compiler_params=pltpu.CompilerParams(vmem_limit_bytes=14 * 1024 * 1024),
    )(hidden, state_gates, state_bias, gain, shift, *vectors, *matrices)


def receive(*operands):
    vmem = pl.BlockSpec(memory_space=pltpu.VMEM)
    return pl.pallas_call(
        receive_kernel,
        out_shape=jax.ShapeDtypeStruct((FACES, 8, 4, 512), f32),
        in_specs=[vmem] * 14,
        out_specs=vmem,
        scratch_shapes=[
            pltpu.VMEM((4096, SIDE), f32),
            pltpu.VMEM((4, 384, 256), bf16),
            pltpu.VMEM((384, 256), f32),
            pltpu.VMEM((384, 1024), bf16),
        ],
        cost_estimate=pl.CostEstimate(
            flops=2 * 700000000, bytes_accessed=8000000, transcendentals=2000000
        ),
        compiler_params=pltpu.CompilerParams(vmem_limit_bytes=20 * 1024 * 1024),
    )(*operands)


def shards(
    features,
    conv_kernel,
    conv_bias,
    neighbour_face,
    neighbour_side,
    norm_gain,
    norm_shift,
    expand_weight,
    expand_bias,
    reduce_weight,
    reduce_bias,
    layer_scale,
    project_weight,
    project_bias,
    input_gates,
    input_bias,
    state_gates,
    state_bias,
    hidden_state,
):
    message = send(features, conv_kernel, conv_bias, neighbour_face, neighbour_side)
    message = message.reshape(128, 32, SIDE)
    arrived = lax.all_to_all(message, ("ty", "tx"), split_axis=0, concat_axis=0, tiled=True)
    row = lambda v: v.reshape(1, -1)
    previous, from_state, gain, shift, *held = ready(
        hidden_state,
        state_gates,
        row(state_bias),
        row(norm_gain),
        row(norm_shift),
        [row(v) for v in (expand_bias, reduce_bias, layer_scale, project_bias, input_bias)],
        [expand_weight, reduce_weight, project_weight, input_gates],
    )
    vectors, matrices = held[:5], held[5:]
    return receive(
        arrived.reshape(4096, SIDE),
        gain,
        shift,
        matrices[0],
        vectors[0],
        matrices[1],
        vectors[1],
        vectors[2],
        matrices[2],
        vectors[3],
        matrices[3],
        vectors[4],
        previous,
        from_state,
    )


def solution(mesh):
    placed = (
        P(("ty", "tx"), None, None, None),
        P(None, ("ty", "tx")),
        P(("ty", "tx")),
        P(),
        P(),
        P(),
        P(),
        P(),
        P(),
        P(),
        P(),
        P(),
        P(),
        P(),
        P(),
        P(),
        P(),
        P(),
        P(None, "ty", "tx", None),
    )
    return jax.shard_map(
        shards, mesh=mesh, in_specs=placed, out_specs=P(None, "ty", "tx", None), check_vma=False
    )
```

```python
import jax
import jax.numpy as jnp
from jax import lax
from jax.experimental import pallas as pl
from jax.experimental.pallas import tpu as pltpu
from jax.sharding import PartitionSpec as P

KERNEL = 7
FACES = 12
SIDE = 128
EPSILON = 1e-06
PADDED = SIDE + 16
DEPTH = (KERNEL + 1) * SIDE

VMEM_LIMIT = 63 * 1024 * 1024
RECEIVE_VMEM = 44 * 1024 * 1024
WEIGHT_ROWS = 8192
STATE_FACES = 34 * FACES

f32 = jnp.float32
bf16 = jnp.bfloat16


def iota(shape, axis):
    return lax.broadcasted_iota(jnp.int32, shape, axis)


def flip_head(tile):
    row = iota(tile.shape, 0)
    return jnp.where(
        row == 7,
        pltpu.roll(tile, 7, 0),
        jnp.where(row == 6, pltpu.roll(tile, 5, 0), pltpu.roll(tile, 3, 0)),
    )


def flip_tail(tile):
    row = iota(tile.shape, 0)
    return jnp.where(
        row == 0,
        pltpu.roll(tile, 1, 0),
        jnp.where(row == 1, pltpu.roll(tile, 3, 0), pltpu.roll(tile, 5, 0)),
    )


def lane_row(shape, axis):
    n = iota(shape, axis)
    return (n & ~15) + ((n & 7) << 1) + ((n >> 3) & 1)


def send_kernel(
    kernel_hbm,
    face_hbm,
    side_hbm,
    bias_hbm,
    x_hbm,
    msg_hbm,
    kernel_ref,
    face_ref,
    side_ref,
    bias_ref,
    x_ref,
    yt_ref,
    strip_ref,
    flip_ref,
    lhs_ref,
    rhs_ref,
    pool_ref,
    out_ref,
    msg_ref,
    small_sem,
    x_sem,
    msg_sem,
):
    loads = [
        pltpu.make_async_copy(source, target, small_sem.at[k])
        for k, (source, target) in enumerate(
            [
                (kernel_hbm, kernel_ref),
                (face_hbm, face_ref),
                (side_hbm, side_ref),
                (bias_hbm, bias_ref),
            ]
        )
    ] + [pltpu.make_async_copy(x_hbm.at[c], x_ref.at[c], x_sem.at[c]) for c in range(2)]
    for copy in loads:
        copy.start()

    i = iota((SIDE, SIDE), 0)
    raw = iota((SIDE, SIDE), 1)
    pair = ((i >> 4) == (raw >> 4)) & (((i >> 1) & 7) == (raw & 7))
    for half in range(2):
        pool_ref[half * SIDE : (half + 1) * SIDE, :] = jnp.where(
            pair & (((raw >> 3) & 1) == half), 0.25, 0.0
        ).astype(bf16)

    row8 = iota((8, SIDE), 0)
    lane8 = iota((8, SIDE), 1)
    at_left = (lane8 == SIDE - 1 - row8) & (row8 < 3)
    at_right = (lane8 == row8) & (row8 < 3)
    lane16 = iota((16, SIDE), 1)
    offset = 64 + iota((16, SIDE), 0) - lane_row((16, SIDE), 1) + 3
    head = lane_row((8, SIDE), 1)
    band = jnp.where(row8 < 4, 2 - row8 - head, SIDE + 3 + (row8 - 4) - head)
    band = jnp.where((row8 & 3) == 3, -1, band)

    for copy in loads:
        copy.wait()

    def store_weights(c, rows, value):
        high = value.astype(bf16)
        rhs_ref[c, rows, :SIDE] = high
        rhs_ref[c, rows, SIDE:] = (value - high.astype(f32)).astype(bf16)

    for c in range(2):
        borders = []
        for q in range(KERNEL):
            base = jnp.zeros((16, SIDE), f32)
            border = jnp.zeros((8, SIDE), f32)
            for p in range(KERNEL):
                weight = kernel_ref[c, p * KERNEL + q]
                base = jnp.where(offset == p, weight, base)
                border = jnp.where(band == p, weight, border)
            for k in range(8):
                value = base if k == 4 else pltpu.roll(base, (16 * (k - 4)) % SIDE, 1)
                if k == 0:
                    value = jnp.where(lane16 >= SIDE - 16, 0.0, value)
                if k == 7:
                    value = jnp.where(lane16 < 16, 0.0, value)
                at = q * SIDE + k * 16
                store_weights(c, slice(at, at + 16), value)
            borders.append(border)
        borders.append(jnp.zeros((SIDE - 8 * KERNEL, SIDE), f32))
        store_weights(c, slice(KERNEL * SIDE, DEPTH), jnp.concatenate(borders, axis=0))

    for c in range(2):

        def prepare(f, c=c):
            x = x_ref[c, f]
            y = x.T.astype(f32)
            x = x.astype(f32)
            yt_ref[c, f, 8 : 8 + SIDE, :] = y
            strip_ref[c, f * 4] = x[:8]
            flip_ref[c, f * 4] = flip_head(x[:8])
            strip_ref[c, f * 4 + 1] = flip_tail(x[SIDE - 8 :])
            flip_ref[c, f * 4 + 1] = x[SIDE - 8 :]
            strip_ref[c, f * 4 + 2] = y[:8]
            flip_ref[c, f * 4 + 2] = flip_head(y[:8])
            strip_ref[c, f * 4 + 3] = flip_tail(y[SIDE - 8 :])
            flip_ref[c, f * 4 + 3] = y[SIDE - 8 :]

        for f in range(FACES):
            prepare(f)

    sends = []
    for c in range(2):

        def assemble(f, c=c):
            at = [face_ref[s, f] * 4 + side_ref[s, f] for s in range(4)]
            left = strip_ref[c, at[2]]
            right = strip_ref[c, at[3]]
            yt_ref[c, f, :8, :] = flip_ref[c, at[2]]
            yt_ref[c, f, 8 + SIDE :, :] = right
            bands = jnp.where(
                row8 < 4, strip_ref[c, at[0]], pltpu.roll(strip_ref[c, at[1]], 4, 0)
            )
            upper = jnp.where(at_left, left[:, :1], 0.0) + jnp.where(at_right, right[:, :1], 0.0)
            lower = jnp.where(at_left, left[:, SIDE - 1 :], 0.0) + jnp.where(
                at_right, right[:, SIDE - 1 :], 0.0
            )
            upper = jnp.sum(upper, axis=0, keepdims=True)
            lower = jnp.sum(lower, axis=0, keepdims=True)
            corner = 0.5 * (
                jnp.where(lane8 >= SIDE // 2, bands[:, :1], bands[:, SIDE - 1 :])
                + jnp.where(row8 < 4, upper, lower)
            )
            shifted = []
            for q in range(KERNEL):
                s = 3 - q
                if s > 0:
                    shifted.append(pltpu.roll(jnp.where(lane8 >= SIDE - s, corner, bands), s, 1))
                elif s < 0:
                    shifted.append(pltpu.roll(jnp.where(lane8 < -s, corner, bands), SIDE + s, 1))
                else:
                    shifted.append(bands)
            shifted.append(jnp.zeros((SIDE - 8 * KERNEL, SIDE), f32))
            rows = slice(f * SIDE, (f + 1) * SIDE)
            lhs_ref[rows, KERNEL * SIDE :] = jnp.concatenate(shifted, axis=0).astype(bf16).T
            for q in range(KERNEL):
                lhs_ref[rows, q * SIDE : (q + 1) * SIDE] = yt_ref[
                    c, f, 5 + q : 5 + q + SIDE, :
                ].astype(bf16)

        for f in range(FACES):
            assemble(f)

        bias = bias_ref[c]
        for part in range(3):
            product = jnp.dot(
                lhs_ref[part * 512 : (part + 1) * 512, :],
                rhs_ref[c],
                preferred_element_type=f32,
            )
            conv = product[:, :SIDE] + product[:, SIDE:] + bias
            for g in range(4):
                f = part * 4 + g
                for t in range(16):
                    at = g * SIDE + t * 8
                    out_ref[t, f * 8 : (f + 1) * 8, :] = conv[at : at + 8]
        middle = slice(3 * SIDE, 4 * SIDE)
        pooled = jnp.dot(
            lhs_ref[: 6 * SIDE, middle], pool_ref[:SIDE, :], preferred_element_type=f32
        ) + jnp.dot(lhs_ref[6 * SIDE :, middle], pool_ref[SIDE:, :], preferred_element_type=f32)
        for f in range(6):
            for t in range(16):
                at = f * SIDE + t * 8
                out_ref[t, 96 + f * 8 : 96 + (f + 1) * 8, :] = pooled[at : at + 8]

        def pack(t, c=c):
            block = jnp.concatenate(
                [
                    out_ref[t, pl.ds(0, 48, stride=2), :],
                    out_ref[t, pl.ds(1, 48, stride=2), :],
                    out_ref[t, pl.ds(96, 24, stride=2), :] + out_ref[t, pl.ds(97, 24, stride=2), :],
                    jnp.zeros((8, SIDE), f32),
                ],
                axis=0,
            )
            block = block.astype(bf16).T
            for ty in range(8):
                msg_ref[ty, t, c * 16 : (c + 1) * 16, :] = block[ty * 16 : (ty + 1) * 16]

        for t in range(16):
            pack(t)
        sends.append(
            pltpu.make_async_copy(
                msg_ref.at[:, :, pl.ds(c * 16, 16)],
                msg_hbm.at[:, :, pl.ds(c * 16, 16)],
                msg_sem.at[c],
            )
        )
        sends[-1].start()
    for copy in sends:
        copy.wait()


def send(features, conv_kernel, conv_bias, neighbour_face, neighbour_side):
    hbm = pl.BlockSpec(memory_space=pl.ANY)
    return pl.pallas_call(
        send_kernel,
        out_shape=jax.ShapeDtypeStruct((8, 16, 32, SIDE), bf16),
        in_specs=[hbm] * 5,
        out_specs=hbm,
        scratch_shapes=[
            pltpu.SMEM((2, KERNEL * KERNEL), f32),
            pltpu.SMEM((4, FACES), jnp.int32),
            pltpu.SMEM((4, FACES), jnp.int32),
            pltpu.SMEM((2,), f32),
            pltpu.VMEM((2, FACES, SIDE, SIDE), bf16),
            pltpu.VMEM((2, FACES, PADDED, SIDE), f32),
            pltpu.VMEM((2, FACES * 4, 8, SIDE), f32),
            pltpu.VMEM((2, FACES * 4, 8, SIDE), f32),
            pltpu.VMEM((FACES * SIDE, DEPTH), bf16),
            pltpu.VMEM((2, DEPTH, 2 * SIDE), bf16),
            pltpu.VMEM((2 * SIDE, SIDE), bf16),
            pltpu.VMEM((16, 144, SIDE), f32),
            pltpu.VMEM((8, 16, 32, SIDE), bf16),
            pltpu.SemaphoreType.DMA((4,)),
            pltpu.SemaphoreType.DMA((2,)),
            pltpu.SemaphoreType.DMA((2,)),
        ],
        cost_estimate=pl.CostEstimate(
            flops=2 * 2 * 1536 * DEPTH * 256, bytes_accessed=4000000, transcendentals=0
        ),
        compiler_params=pltpu.CompilerParams(vmem_limit_bytes=VMEM_LIMIT),
    )(conv_kernel.T, neighbour_face.T, neighbour_side.T, conv_bias, features)


def receive_kernel(
    msg_ref,
    vector_ref,
    from_state_ref,
    weight_hbm,
    held_hbm,
    out_hbm,
    expand_ref,
    reduce_ref,
    project_ref,
    input_ref,
    hidden_ref,
    out_ref,
    wide_ref,
    normed_ref,
    pooled_ref,
    units_ref,
    sems,
    out_sem,
):
    operands = [
        (expand_part(weight_hbm), expand_ref),
        (reduce_part(weight_hbm), reduce_ref),
        (project_part(weight_hbm), project_ref),
        (input_part(weight_hbm), input_ref),
        (held_hbm.at[pl.ds(0, FACES)], hidden_ref),
    ]
    loads = [
        pltpu.make_async_copy(source, target, sems.at[k])
        for k, (source, target) in enumerate(operands)
    ]
    for copy in loads:
        copy.start()

    def vector(k, lanes):
        return vector_ref[k : k + 1, lanes]

    def column(k):
        row = vector(k, slice(0, 256))
        halves = [row[:, :SIDE], row[:, SIDE:]]
        return jnp.concatenate([jnp.broadcast_to(v, (SIDE, SIDE)).T for v in halves], axis=0)

    gain = column(5)
    shift = column(6)
    wide_ref[...] = msg_ref[...].astype(f32)
    lane = iota((256, SIDE), 1)
    for r in range(16):
        di, ci = r // 8, r % 8
        values = wide_ref[pl.ds(r, 256, stride=16), :]
        center = jnp.sum(values, axis=0, keepdims=True) * (1.0 / 256)
        away = values - center
        spread = jnp.sum(away * away, axis=0, keepdims=True) * (1.0 / 256)
        normed = away * lax.rsqrt(spread + EPSILON) * gain + shift
        cells = jnp.where(lane < 96, normed, values).astype(bf16).T
        rows = slice(ci * 48, (ci + 1) * 48)
        normed_ref[di * 2, rows, :] = cells[:48]
        normed_ref[di * 2 + 1, rows, :] = cells[48:96]
        pooled_ref[ci * 48 + di * 24 : ci * 48 + (di + 1) * 24, :] = cells[96:].astype(f32)[:24]

    loads[0].wait()
    for k in range(4):
        lanes = slice(k * 256, (k + 1) * 256)
        for m in range(3):
            rows = slice(m * 128, (m + 1) * 128)
            hidden = jnp.dot(
                normed_ref[:, rows, :].reshape(512, 256),
                expand_ref[:, lanes],
                preferred_element_type=f32,
            )
            total = None
            for s in range(4):
                part = hidden[s * 128 : (s + 1) * 128] + vector(0, lanes)
                unit = part * (1.0 + lax.erf(part * (0.5**0.5)))
                total = unit if total is None else total + unit
            units_ref[rows, lanes] = total.astype(bf16)

    loads[1].wait()
    loads[2].wait()
    update = (
        jnp.dot(units_ref[...], reduce_ref[...], preferred_element_type=f32) * 0.125
        + vector(1, slice(0, 256))
    ) * vector(2, slice(0, 256))
    pooled = (pooled_ref[...] + update).astype(bf16)
    mapped = (
        jnp.dot(pooled, project_ref[...], preferred_element_type=f32) + vector(3, slice(0, 512))
    ).astype(bf16)

    for copy in loads[3:]:
        copy.wait()

    def sigmoid(v):
        return 0.5 * jnp.tanh(0.5 * v) + 0.5

    for k in range(2):

        def gate(block):
            lanes = slice(block * 512 + k * 256, block * 512 + (k + 1) * 256)
            return (
                jnp.dot(mapped, input_ref[:, lanes], preferred_element_type=f32)
                + vector(4, lanes),
                from_state_ref[:, lanes],
            )

        lanes = slice(k * 256, (k + 1) * 256)
        a, b = gate(0)
        update_gate = sigmoid(a + b)
        a, b = gate(1)
        reset_gate = sigmoid(a + b)
        a, b = gate(2)
        candidate = jnp.tanh(a + reset_gate * b)
        for ci in range(8):
            for f in range(FACES):
                rows = slice(ci * 48 + f * 4, ci * 48 + f * 4 + 4)
                kept = candidate[rows]
                out_ref[f, ci, :, lanes] = kept + update_gate[rows] * (
                    hidden_ref[f, ci, :, lanes] - kept
                )
    copy = pltpu.make_async_copy(out_ref, out_hbm, out_sem)
    copy.start()
    copy.wait()


def input_part(ref):
    return ref.at[pl.ds(0, 512)]


def expand_part(ref):
    return ref.at[pl.ds(512, 256), pl.ds(0, 1024)]


def project_part(ref):
    return ref.at[pl.ds(512, 256), pl.ds(1024, 512)]


def reduce_part(ref):
    return ref.at[pl.ds(768, 1024), pl.ds(0, 256)]


def ready_kernel(
    hidden_hbm,
    state_hbm,
    state_bias_hbm,
    gain_hbm,
    shift_hbm,
    expand_bias_hbm,
    reduce_bias_hbm,
    scale_hbm,
    project_bias_hbm,
    input_bias_hbm,
    expand_hbm,
    reduce_hbm,
    project_hbm,
    input_hbm,
    from_state_ref,
    vector_ref,
    weight_hbm,
    held_hbm,
    hidden_ref,
    state_ref,
    state_bias_ref,
    gain_ref,
    shift_ref,
    expand_bias_ref,
    reduce_bias_ref,
    scale_ref,
    project_bias_ref,
    input_bias_ref,
    previous_ref,
    sems,
    pack_sems,
):
    packs = [
        pltpu.make_async_copy(source, target, pack_sems.at[k])
        for k, (source, target) in enumerate(
            [
                (expand_hbm, expand_part(weight_hbm)),
                (reduce_hbm, reduce_part(weight_hbm)),
                (project_hbm, project_part(weight_hbm)),
                (input_hbm, input_part(weight_hbm)),
                (hidden_hbm, held_hbm.at[pl.ds(0, FACES)]),
            ]
        )
    ]
    for copy in packs:
        copy.start()
    operands = [
        (hidden_hbm, hidden_ref),
        (state_hbm, state_ref),
        (state_bias_hbm, state_bias_ref),
        (gain_hbm, gain_ref),
        (shift_hbm, shift_ref),
        (expand_bias_hbm, expand_bias_ref),
        (reduce_bias_hbm, reduce_bias_ref),
        (scale_hbm, scale_ref),
        (project_bias_hbm, project_bias_ref),
        (input_bias_hbm, input_bias_ref),
    ]
    loads = [
        pltpu.make_async_copy(source, target, sems.at[k])
        for k, (source, target) in enumerate(operands)
    ]
    for copy in loads:
        copy.start()
    for copy in loads:
        copy.wait()
    for ci in range(8):
        for f in range(FACES):
            at = ci * 48 + f * 4
            previous_ref[at : at + 4, :] = hidden_ref[f, ci]
    for k in range(6):
        lanes = slice(k * 256, (k + 1) * 256)
        from_state_ref[:, lanes] = (
            jnp.dot(
                previous_ref[...].astype(bf16), state_ref[:, lanes], preferred_element_type=f32
            )
            + state_bias_ref[:, lanes]
        )
    vectors = (
        expand_bias_ref,
        reduce_bias_ref,
        scale_ref,
        project_bias_ref,
        input_bias_ref,
        gain_ref,
        shift_ref,
    )
    for k, source in enumerate(vectors):
        vector_ref[k : k + 1, : source.shape[1]] = source[...]
    for copy in packs:
        copy.wait()


def ready(hidden, state_gates, vectors, weights):
    vmem = pl.BlockSpec(memory_space=pltpu.VMEM)
    hbm = pl.BlockSpec(memory_space=pl.ANY)
    operands = (hidden, state_gates) + tuple(v.reshape(1, -1) for v in vectors)
    return pl.pallas_call(
        ready_kernel,
        out_shape=(
            jax.ShapeDtypeStruct((384, 1536), f32),
            jax.ShapeDtypeStruct((8, 1536), f32),
            jax.ShapeDtypeStruct((WEIGHT_ROWS, 1536), bf16),
            jax.ShapeDtypeStruct((STATE_FACES, 8, 4, 512), f32),
        ),
        in_specs=[hbm] * (len(operands) + len(weights)),
        out_specs=(vmem, vmem, hbm, hbm),
        scratch_shapes=[pltpu.VMEM(v.shape, v.dtype) for v in operands]
        + [
            pltpu.VMEM((384, 512), f32),
            pltpu.SemaphoreType.DMA((len(operands),)),
            pltpu.SemaphoreType.DMA((5,)),
        ],
        cost_estimate=pl.CostEstimate(
            flops=2 * 384 * 512 * 1536, bytes_accessed=8000000, transcendentals=0
        ),
        compiler_params=pltpu.CompilerParams(vmem_limit_bytes=RECEIVE_VMEM),
    )(*operands, *weights)


def receive(message, vectors, from_state, weights, held):
    vmem = pl.BlockSpec(memory_space=pltpu.VMEM)
    hbm = pl.BlockSpec(memory_space=pl.ANY)
    result = jax.ShapeDtypeStruct((FACES, 8, 4, 512), f32)
    return pl.pallas_call(
        receive_kernel,
        out_shape=result,
        in_specs=[vmem, vmem, vmem, hbm, hbm],
        out_specs=hbm,
        scratch_shapes=[
            pltpu.VMEM((256, 1024), bf16),
            pltpu.VMEM((1024, 256), bf16),
            pltpu.VMEM((256, 512), bf16),
            pltpu.VMEM((512, 1536), bf16),
            pltpu.VMEM(result.shape, f32),
            pltpu.VMEM(result.shape, f32),
            pltpu.VMEM((4096, SIDE), f32),
            pltpu.VMEM((4, 384, 256), bf16),
            pltpu.VMEM((384, 256), f32),
            pltpu.VMEM((384, 1024), bf16),
            pltpu.SemaphoreType.DMA((5,)),
            pltpu.SemaphoreType.DMA,
        ],
        cost_estimate=pl.CostEstimate(
            flops=2 * 700000000, bytes_accessed=8000000, transcendentals=2000000
        ),
        compiler_params=pltpu.CompilerParams(vmem_limit_bytes=RECEIVE_VMEM),
    )(message, vectors, from_state, weights, held)


def shards(
    features,
    conv_kernel,
    conv_bias,
    neighbour_face,
    neighbour_side,
    norm_gain,
    norm_shift,
    expand_weight,
    expand_bias,
    reduce_weight,
    reduce_bias,
    layer_scale,
    project_weight,
    project_bias,
    input_gates,
    input_bias,
    state_gates,
    state_bias,
    hidden_state,
):
    message = send(features, conv_kernel, conv_bias, neighbour_face, neighbour_side)
    message = message.reshape(128, 32, SIDE)
    arrived = lax.all_to_all(message, ("ty", "tx"), split_axis=0, concat_axis=0, tiled=True)
    from_state, vectors, weights, held = ready(
        hidden_state,
        state_gates,
        (
            state_bias,
            norm_gain,
            norm_shift,
            expand_bias,
            reduce_bias,
            layer_scale,
            project_bias,
            input_bias,
        ),
        (expand_weight, reduce_weight, project_weight, input_gates),
    )
    return receive(arrived.reshape(4096, SIDE), vectors, from_state, weights, held)


def solution(mesh):
    placed = (
        P(("ty", "tx"), None, None, None),
        P(None, ("ty", "tx")),
        P(("ty", "tx")),
        P(),
        P(),
        P(),
        P(),
        P(),
        P(),
        P(),
        P(),
        P(),
        P(),
        P(),
        P(),
        P(),
        P(),
        P(),
        P(None, "ty", "tx", None),
    )
    return jax.shard_map(
        shards, mesh=mesh, in_specs=placed, out_specs=P(None, "ty", "tx", None), check_vma=False
    )
```

```python
import jax
import jax.numpy as jnp
from jax import lax
from jax.experimental import pallas as pl
from jax.experimental.pallas import tpu as pltpu
from jax.sharding import PartitionSpec as P

KERNEL = 7
FACES = 12
SIDE = 128
EPSILON = 1e-06
PADDED = SIDE + 16
DEPTH = (KERNEL + 1) * SIDE

VMEM_LIMIT = 63 * 1024 * 1024
READY_VMEM = 52 * 1024 * 1024
RECEIVE_VMEM = 44 * 1024 * 1024
WEIGHT_ROWS = 8192
STATE_FACES = 34 * FACES
STATE_ROWS = 4096

f32 = jnp.float32
bf16 = jnp.bfloat16


def iota(shape, axis):
    return lax.broadcasted_iota(jnp.int32, shape, axis)


def flip_head(tile):
    row = iota(tile.shape, 0)
    return jnp.where(
        row == 7,
        pltpu.roll(tile, 7, 0),
        jnp.where(row == 6, pltpu.roll(tile, 5, 0), pltpu.roll(tile, 3, 0)),
    )


def flip_tail(tile):
    row = iota(tile.shape, 0)
    return jnp.where(
        row == 0,
        pltpu.roll(tile, 1, 0),
        jnp.where(row == 1, pltpu.roll(tile, 3, 0), pltpu.roll(tile, 5, 0)),
    )


def lane_row(shape, axis):
    n = iota(shape, axis)
    return (n & ~15) + ((n & 7) << 1) + ((n >> 3) & 1)


def send_kernel(
    kernel_hbm,
    face_hbm,
    side_hbm,
    bias_hbm,
    x_hbm,
    msg_hbm,
    kernel_ref,
    face_ref,
    side_ref,
    bias_ref,
    x_ref,
    yt_ref,
    strip_ref,
    flip_ref,
    lhs_ref,
    rhs_ref,
    pool_ref,
    out_ref,
    msg_ref,
    small_sem,
    x_sem,
    msg_sem,
):
    loads = [
        pltpu.make_async_copy(source, target, small_sem.at[k])
        for k, (source, target) in enumerate(
            [
                (kernel_hbm, kernel_ref),
                (face_hbm, face_ref),
                (side_hbm, side_ref),
                (bias_hbm, bias_ref),
            ]
        )
    ] + [pltpu.make_async_copy(x_hbm.at[c], x_ref.at[c], x_sem.at[c]) for c in range(2)]
    for copy in loads:
        copy.start()

    i = iota((SIDE, SIDE), 0)
    raw = iota((SIDE, SIDE), 1)
    pair = ((i >> 4) == (raw >> 4)) & (((i >> 1) & 7) == (raw & 7))
    for half in range(2):
        pool_ref[half * SIDE : (half + 1) * SIDE, :] = jnp.where(
            pair & (((raw >> 3) & 1) == half), 0.25, 0.0
        ).astype(bf16)

    row8 = iota((8, SIDE), 0)
    lane8 = iota((8, SIDE), 1)
    at_left = (lane8 == SIDE - 1 - row8) & (row8 < 3)
    at_right = (lane8 == row8) & (row8 < 3)
    lane16 = iota((16, SIDE), 1)
    offset = 64 + iota((16, SIDE), 0) - lane_row((16, SIDE), 1) + 3
    head = lane_row((8, SIDE), 1)
    band = jnp.where(row8 < 4, 2 - row8 - head, SIDE + 3 + (row8 - 4) - head)
    band = jnp.where((row8 & 3) == 3, -1, band)

    for copy in loads:
        copy.wait()

    def store_weights(c, rows, value):
        high = value.astype(bf16)
        rhs_ref[c, rows, :SIDE] = high
        rhs_ref[c, rows, SIDE:] = (value - high.astype(f32)).astype(bf16)

    for c in range(2):
        borders = []
        for q in range(KERNEL):
            base = jnp.zeros((16, SIDE), f32)
            border = jnp.zeros((8, SIDE), f32)
            for p in range(KERNEL):
                weight = kernel_ref[c, p * KERNEL + q]
                base = jnp.where(offset == p, weight, base)
                border = jnp.where(band == p, weight, border)
            for k in range(8):
                value = base if k == 4 else pltpu.roll(base, (16 * (k - 4)) % SIDE, 1)
                if k == 0:
                    value = jnp.where(lane16 >= SIDE - 16, 0.0, value)
                if k == 7:
                    value = jnp.where(lane16 < 16, 0.0, value)
                at = q * SIDE + k * 16
                store_weights(c, slice(at, at + 16), value)
            borders.append(border)
        borders.append(jnp.zeros((SIDE - 8 * KERNEL, SIDE), f32))
        store_weights(c, slice(KERNEL * SIDE, DEPTH), jnp.concatenate(borders, axis=0))

    for c in range(2):

        def prepare(f, c=c):
            x = x_ref[c, f]
            y = x.T.astype(f32)
            x = x.astype(f32)
            yt_ref[c, f, 8 : 8 + SIDE, :] = y
            strip_ref[c, f * 4] = x[:8]
            flip_ref[c, f * 4] = flip_head(x[:8])
            strip_ref[c, f * 4 + 1] = flip_tail(x[SIDE - 8 :])
            flip_ref[c, f * 4 + 1] = x[SIDE - 8 :]
            strip_ref[c, f * 4 + 2] = y[:8]
            flip_ref[c, f * 4 + 2] = flip_head(y[:8])
            strip_ref[c, f * 4 + 3] = flip_tail(y[SIDE - 8 :])
            flip_ref[c, f * 4 + 3] = y[SIDE - 8 :]

        for f in range(FACES):
            prepare(f)

    sends = []
    for c in range(2):

        def assemble(f, c=c):
            at = [face_ref[s, f] * 4 + side_ref[s, f] for s in range(4)]
            left = strip_ref[c, at[2]]
            right = strip_ref[c, at[3]]
            yt_ref[c, f, :8, :] = flip_ref[c, at[2]]
            yt_ref[c, f, 8 + SIDE :, :] = right
            bands = jnp.where(
                row8 < 4, strip_ref[c, at[0]], pltpu.roll(strip_ref[c, at[1]], 4, 0)
            )
            upper = jnp.where(at_left, left[:, :1], 0.0) + jnp.where(at_right, right[:, :1], 0.0)
            lower = jnp.where(at_left, left[:, SIDE - 1 :], 0.0) + jnp.where(
                at_right, right[:, SIDE - 1 :], 0.0
            )
            upper = jnp.sum(upper, axis=0, keepdims=True)
            lower = jnp.sum(lower, axis=0, keepdims=True)
            corner = 0.5 * (
                jnp.where(lane8 >= SIDE // 2, bands[:, :1], bands[:, SIDE - 1 :])
                + jnp.where(row8 < 4, upper, lower)
            )
            shifted = []
            for q in range(KERNEL):
                s = 3 - q
                if s > 0:
                    shifted.append(pltpu.roll(jnp.where(lane8 >= SIDE - s, corner, bands), s, 1))
                elif s < 0:
                    shifted.append(pltpu.roll(jnp.where(lane8 < -s, corner, bands), SIDE + s, 1))
                else:
                    shifted.append(bands)
            shifted.append(jnp.zeros((SIDE - 8 * KERNEL, SIDE), f32))
            rows = slice(f * SIDE, (f + 1) * SIDE)
            lhs_ref[rows, KERNEL * SIDE :] = jnp.concatenate(shifted, axis=0).astype(bf16).T
            for q in range(KERNEL):
                lhs_ref[rows, q * SIDE : (q + 1) * SIDE] = yt_ref[
                    c, f, 5 + q : 5 + q + SIDE, :
                ].astype(bf16)

        for f in range(FACES):
            assemble(f)

        bias = bias_ref[c]
        for part in range(3):
            product = jnp.dot(
                lhs_ref[part * 512 : (part + 1) * 512, :],
                rhs_ref[c],
                preferred_element_type=f32,
            )
            conv = product[:, :SIDE] + product[:, SIDE:] + bias
            for g in range(4):
                f = part * 4 + g
                for t in range(16):
                    at = g * SIDE + t * 8
                    out_ref[t, f * 8 : (f + 1) * 8, :] = conv[at : at + 8]
        middle = slice(3 * SIDE, 4 * SIDE)
        pooled = jnp.dot(
            lhs_ref[: 6 * SIDE, middle], pool_ref[:SIDE, :], preferred_element_type=f32
        ) + jnp.dot(lhs_ref[6 * SIDE :, middle], pool_ref[SIDE:, :], preferred_element_type=f32)
        for f in range(6):
            for t in range(16):
                at = f * SIDE + t * 8
                out_ref[t, 96 + f * 8 : 96 + (f + 1) * 8, :] = pooled[at : at + 8]

        def pack(t, c=c):
            block = jnp.concatenate(
                [
                    out_ref[t, pl.ds(0, 48, stride=2), :],
                    out_ref[t, pl.ds(1, 48, stride=2), :],
                    out_ref[t, pl.ds(96, 24, stride=2), :] + out_ref[t, pl.ds(97, 24, stride=2), :],
                    jnp.zeros((8, SIDE), f32),
                ],
                axis=0,
            )
            block = block.astype(bf16).T
            for ty in range(8):
                msg_ref[ty, t, c * 16 : (c + 1) * 16, :] = block[ty * 16 : (ty + 1) * 16]

        for t in range(16):
            pack(t)
        sends.append(
            pltpu.make_async_copy(
                msg_ref.at[:, :, pl.ds(c * 16, 16)],
                msg_hbm.at[:, :, pl.ds(c * 16, 16)],
                msg_sem.at[c],
            )
        )
        sends[-1].start()
    for copy in sends:
        copy.wait()


def send(features, conv_kernel, conv_bias, neighbour_face, neighbour_side):
    hbm = pl.BlockSpec(memory_space=pl.ANY)
    return pl.pallas_call(
        send_kernel,
        out_shape=jax.ShapeDtypeStruct((8, 16, 32, SIDE), bf16),
        in_specs=[hbm] * 5,
        out_specs=hbm,
        scratch_shapes=[
            pltpu.SMEM((2, KERNEL * KERNEL), f32),
            pltpu.SMEM((4, FACES), jnp.int32),
            pltpu.SMEM((4, FACES), jnp.int32),
            pltpu.SMEM((2,), f32),
            pltpu.VMEM((2, FACES, SIDE, SIDE), bf16),
            pltpu.VMEM((2, FACES, PADDED, SIDE), f32),
            pltpu.VMEM((2, FACES * 4, 8, SIDE), f32),
            pltpu.VMEM((2, FACES * 4, 8, SIDE), f32),
            pltpu.VMEM((FACES * SIDE, DEPTH), bf16),
            pltpu.VMEM((2, DEPTH, 2 * SIDE), bf16),
            pltpu.VMEM((2 * SIDE, SIDE), bf16),
            pltpu.VMEM((16, 144, SIDE), f32),
            pltpu.VMEM((8, 16, 32, SIDE), bf16),
            pltpu.SemaphoreType.DMA((4,)),
            pltpu.SemaphoreType.DMA((2,)),
            pltpu.SemaphoreType.DMA((2,)),
        ],
        cost_estimate=pl.CostEstimate(
            flops=2 * 2 * 1536 * DEPTH * 256, bytes_accessed=4000000, transcendentals=0
        ),
        compiler_params=pltpu.CompilerParams(vmem_limit_bytes=VMEM_LIMIT),
    )(conv_kernel.T, neighbour_face.T, neighbour_side.T, conv_bias, features)


def receive_kernel(
    msg_ref,
    vector_ref,
    expand_ref,
    reduce_ref,
    project_ref,
    weight_hbm,
    state_hbm,
    held_hbm,
    out_hbm,
    input_ref,
    from_state_ref,
    hidden_ref,
    out_ref,
    wide_ref,
    normed_ref,
    pooled_ref,
    units_ref,
    sems,
    out_sem,
):
    operands = [
        (weight_hbm.at[pl.ds(0, 512)], input_ref),
        (state_hbm.at[pl.ds(0, 384)], from_state_ref),
        (held_hbm.at[pl.ds(0, FACES)], hidden_ref),
    ]
    loads = [
        pltpu.make_async_copy(source, target, sems.at[k])
        for k, (source, target) in enumerate(operands)
    ]
    for copy in loads:
        copy.start()

    def vector(k, lanes):
        return vector_ref[k : k + 1, lanes]

    def column(k):
        row = vector(k, slice(0, 256))
        halves = [row[:, :SIDE], row[:, SIDE:]]
        return jnp.concatenate([jnp.broadcast_to(v, (SIDE, SIDE)).T for v in halves], axis=0)

    gain = column(5)
    shift = column(6)
    wide_ref[...] = msg_ref[...].astype(f32)
    lane = iota((256, SIDE), 1)
    for r in range(16):
        di, ci = r // 8, r % 8
        values = wide_ref[pl.ds(r, 256, stride=16), :]
        center = jnp.sum(values, axis=0, keepdims=True) * (1.0 / 256)
        away = values - center
        spread = jnp.sum(away * away, axis=0, keepdims=True) * (1.0 / 256)
        normed = away * lax.rsqrt(spread + EPSILON) * gain + shift
        cells = jnp.where(lane < 96, normed, values).astype(bf16).T
        rows = slice(ci * 48, (ci + 1) * 48)
        normed_ref[di * 2, rows, :] = cells[:48]
        normed_ref[di * 2 + 1, rows, :] = cells[48:96]
        pooled_ref[ci * 48 + di * 24 : ci * 48 + (di + 1) * 24, :] = cells[96:].astype(f32)[:24]

    for k in range(4):
        lanes = slice(k * 256, (k + 1) * 256)
        for m in range(3):
            rows = slice(m * 128, (m + 1) * 128)
            hidden = jnp.dot(
                normed_ref[:, rows, :].reshape(512, 256),
                expand_ref[:, lanes],
                preferred_element_type=f32,
            )
            total = None
            for s in range(4):
                part = hidden[s * 128 : (s + 1) * 128] + vector(0, lanes)
                unit = part * (1.0 + lax.erf(part * (0.5**0.5)))
                total = unit if total is None else total + unit
            units_ref[rows, lanes] = total.astype(bf16)

    update = (
        jnp.dot(units_ref[...], reduce_ref[...], preferred_element_type=f32) * 0.125
        + vector(1, slice(0, 256))
    ) * vector(2, slice(0, 256))
    pooled = (pooled_ref[...] + update).astype(bf16)
    mapped = (
        jnp.dot(pooled, project_ref[...], preferred_element_type=f32) + vector(3, slice(0, 512))
    ).astype(bf16)

    for copy in loads:
        copy.wait()

    def sigmoid(v):
        return 0.5 * jnp.tanh(0.5 * v) + 0.5

    sends = []
    for k in range(2):

        def gate(block):
            lanes = slice(block * 512 + k * 256, block * 512 + (k + 1) * 256)
            return (
                jnp.dot(mapped, input_ref[:, lanes], preferred_element_type=f32)
                + vector(4, lanes),
                from_state_ref[:, lanes],
            )

        lanes = slice(k * 256, (k + 1) * 256)
        a, b = gate(0)
        update_gate = sigmoid(a + b)
        a, b = gate(1)
        reset_gate = sigmoid(a + b)
        a, b = gate(2)
        candidate = jnp.tanh(a + reset_gate * b)
        for ci in range(8):
            for f in range(FACES):
                rows = slice(ci * 48 + f * 4, ci * 48 + f * 4 + 4)
                kept = candidate[rows]
                out_ref[f, ci, :, lanes] = kept + update_gate[rows] * (
                    hidden_ref[f, ci, :, lanes] - kept
                )
        sends.append(
            pltpu.make_async_copy(
                out_ref.at[:, :, :, lanes], out_hbm.at[:, :, :, lanes], out_sem.at[k]
            )
        )
        sends[-1].start()
    for copy in sends:
        copy.wait()


def ready_kernel(
    hidden_hbm,
    state_hbm,
    state_bias_hbm,
    gain_hbm,
    shift_hbm,
    expand_bias_hbm,
    reduce_bias_hbm,
    scale_hbm,
    project_bias_hbm,
    input_bias_hbm,
    expand_hbm,
    reduce_hbm,
    project_hbm,
    input_hbm,
    vector_ref,
    expand_ref,
    reduce_ref,
    project_ref,
    weight_hbm,
    state_part_hbm,
    held_hbm,
    hidden_ref,
    state_ref,
    state_bias_ref,
    gain_ref,
    shift_ref,
    expand_bias_ref,
    reduce_bias_ref,
    scale_ref,
    project_bias_ref,
    input_bias_ref,
    previous_ref,
    from_state_ref,
    input_ref,
    sems,
    pack_sems,
):
    packs = [
        pltpu.make_async_copy(source, target, pack_sems.at[k])
        for k, (source, target) in enumerate(
            [
                (expand_hbm, expand_ref),
                (reduce_hbm, reduce_ref),
                (project_hbm, project_ref),
                (input_hbm, input_ref),
            ]
        )
    ]
    for copy in packs:
        copy.start()
    operands = [
        (hidden_hbm, hidden_ref),
        (state_hbm, state_ref),
        (state_bias_hbm, state_bias_ref),
        (gain_hbm, gain_ref),
        (shift_hbm, shift_ref),
        (expand_bias_hbm, expand_bias_ref),
        (reduce_bias_hbm, reduce_bias_ref),
        (scale_hbm, scale_ref),
        (project_bias_hbm, project_bias_ref),
        (input_bias_hbm, input_bias_ref),
    ]
    loads = [
        pltpu.make_async_copy(source, target, sems.at[k])
        for k, (source, target) in enumerate(operands)
    ]
    for copy in loads:
        copy.start()
    for copy in loads + packs:
        copy.wait()
    packs = [
        pltpu.make_async_copy(source, target, pack_sems.at[4 + k])
        for k, (source, target) in enumerate(
            [
                (input_ref, weight_hbm.at[pl.ds(0, 512)]),
                (hidden_ref, held_hbm.at[pl.ds(0, FACES)]),
            ]
        )
    ]
    for copy in packs:
        copy.start()
    for ci in range(8):
        for f in range(FACES):
            at = ci * 48 + f * 4
            previous_ref[at : at + 4, :] = hidden_ref[f, ci]
    for k in range(6):
        lanes = slice(k * 256, (k + 1) * 256)
        from_state_ref[:, lanes] = (
            jnp.dot(
                previous_ref[...].astype(bf16), state_ref[:, lanes], preferred_element_type=f32
            )
            + state_bias_ref[:, lanes]
        )
    packs.append(
        pltpu.make_async_copy(
            from_state_ref, state_part_hbm.at[pl.ds(0, 384)], pack_sems.at[6]
        )
    )
    packs[-1].start()
    vectors = (
        expand_bias_ref,
        reduce_bias_ref,
        scale_ref,
        project_bias_ref,
        input_bias_ref,
        gain_ref,
        shift_ref,
    )
    for k, source in enumerate(vectors):
        vector_ref[k : k + 1, : source.shape[1]] = source[...]
    for copy in packs:
        copy.wait()


def ready(hidden, state_gates, vectors, weights):
    vmem = pl.BlockSpec(memory_space=pltpu.VMEM)
    hbm = pl.BlockSpec(memory_space=pl.ANY)
    operands = (hidden, state_gates) + tuple(v.reshape(1, -1) for v in vectors)
    return pl.pallas_call(
        ready_kernel,
        out_shape=(
            jax.ShapeDtypeStruct((8, 1536), f32),
            *(jax.ShapeDtypeStruct(v.shape, v.dtype) for v in weights[:3]),
            jax.ShapeDtypeStruct((WEIGHT_ROWS, 1536), bf16),
            jax.ShapeDtypeStruct((STATE_ROWS, 1536), f32),
            jax.ShapeDtypeStruct((STATE_FACES, 8, 4, 512), f32),
        ),
        in_specs=[hbm] * (len(operands) + len(weights)),
        out_specs=(vmem,) * 4 + (hbm,) * 3,
        scratch_shapes=[pltpu.VMEM(v.shape, v.dtype) for v in operands]
        + [
            pltpu.VMEM((384, 512), f32),
            pltpu.VMEM((384, 1536), f32),
            pltpu.VMEM((512, 1536), bf16),
            pltpu.SemaphoreType.DMA((len(operands),)),
            pltpu.SemaphoreType.DMA((7,)),
        ],
        cost_estimate=pl.CostEstimate(
            flops=2 * 384 * 512 * 1536, bytes_accessed=8000000, transcendentals=0
        ),
        compiler_params=pltpu.CompilerParams(vmem_limit_bytes=READY_VMEM),
    )(*operands, *weights)


def receive(*operands):
    vmem = pl.BlockSpec(memory_space=pltpu.VMEM)
    hbm = pl.BlockSpec(memory_space=pl.ANY)
    result = jax.ShapeDtypeStruct((FACES, 8, 4, 512), f32)
    return pl.pallas_call(
        receive_kernel,
        out_shape=result,
        in_specs=[vmem] * 5 + [hbm] * 3,
        out_specs=hbm,
        scratch_shapes=[
            pltpu.VMEM((512, 1536), bf16),
            pltpu.VMEM((384, 1536), f32),
            pltpu.VMEM(result.shape, f32),
            pltpu.VMEM(result.shape, f32),
            pltpu.VMEM((4096, SIDE), f32),
            pltpu.VMEM((4, 384, 256), bf16),
            pltpu.VMEM((384, 256), f32),
            pltpu.VMEM((384, 1024), bf16),
            pltpu.SemaphoreType.DMA((3,)),
            pltpu.SemaphoreType.DMA((2,)),
        ],
        cost_estimate=pl.CostEstimate(
            flops=2 * 700000000, bytes_accessed=8000000, transcendentals=2000000
        ),
        compiler_params=pltpu.CompilerParams(vmem_limit_bytes=RECEIVE_VMEM),
    )(*operands)


def shards(
    features,
    conv_kernel,
    conv_bias,
    neighbour_face,
    neighbour_side,
    norm_gain,
    norm_shift,
    expand_weight,
    expand_bias,
    reduce_weight,
    reduce_bias,
    layer_scale,
    project_weight,
    project_bias,
    input_gates,
    input_bias,
    state_gates,
    state_bias,
    hidden_state,
):
    message = send(features, conv_kernel, conv_bias, neighbour_face, neighbour_side)
    message = message.reshape(128, 32, SIDE)
    arrived = lax.all_to_all(message, ("ty", "tx"), split_axis=0, concat_axis=0, tiled=True)
    operands = ready(
        hidden_state,
        state_gates,
        (
            state_bias,
            norm_gain,
            norm_shift,
            expand_bias,
            reduce_bias,
            layer_scale,
            project_bias,
            input_bias,
        ),
        (expand_weight, reduce_weight, project_weight, input_gates),
    )
    return receive(arrived.reshape(4096, SIDE), *operands)


def solution(mesh):
    placed = (
        P(("ty", "tx"), None, None, None),
        P(None, ("ty", "tx")),
        P(("ty", "tx")),
        P(),
        P(),
        P(),
        P(),
        P(),
        P(),
        P(),
        P(),
        P(),
        P(),
        P(),
        P(),
        P(),
        P(),
        P(),
        P(None, "ty", "tx", None),
    )
    return jax.shard_map(
        shards, mesh=mesh, in_specs=placed, out_specs=P(None, "ty", "tx", None), check_vma=False
    )
```

```python
import jax
import jax.numpy as jnp
from jax import lax
from jax.experimental import pallas as pl
from jax.experimental.pallas import tpu as pltpu
from jax.sharding import PartitionSpec as P

KERNEL = 7
FACES = 12
SIDE = 128
EPSILON = 1e-06
PADDED = SIDE + 16
DEPTH = (KERNEL + 1) * SIDE

VMEM_LIMIT = 63 * 1024 * 1024
READY_VMEM = 52 * 1024 * 1024
RECEIVE_VMEM = 44 * 1024 * 1024
WEIGHT_ROWS = 8192
STATE_FACES = 34 * FACES
STATE_ROWS = 4096

f32 = jnp.float32
bf16 = jnp.bfloat16


def iota(shape, axis):
    return lax.broadcasted_iota(jnp.int32, shape, axis)


def flip_head(tile):
    row = iota(tile.shape, 0)
    return jnp.where(
        row == 7,
        pltpu.roll(tile, 7, 0),
        jnp.where(row == 6, pltpu.roll(tile, 5, 0), pltpu.roll(tile, 3, 0)),
    )


def flip_tail(tile):
    row = iota(tile.shape, 0)
    return jnp.where(
        row == 0,
        pltpu.roll(tile, 1, 0),
        jnp.where(row == 1, pltpu.roll(tile, 3, 0), pltpu.roll(tile, 5, 0)),
    )


def lane_row(shape, axis):
    n = iota(shape, axis)
    return (n & ~15) + ((n & 7) << 1) + ((n >> 3) & 1)


def send_kernel(
    kernel_hbm,
    face_hbm,
    side_hbm,
    bias_hbm,
    x_hbm,
    msg_hbm,
    kernel_ref,
    face_ref,
    side_ref,
    bias_ref,
    x_ref,
    yt_ref,
    strip_ref,
    flip_ref,
    lhs_ref,
    rhs_ref,
    pool_ref,
    out_ref,
    msg_ref,
    small_sem,
    x_sem,
    msg_sem,
):
    loads = [
        pltpu.make_async_copy(source, target, small_sem.at[k])
        for k, (source, target) in enumerate(
            [
                (kernel_hbm, kernel_ref),
                (face_hbm, face_ref),
                (side_hbm, side_ref),
                (bias_hbm, bias_ref),
            ]
        )
    ] + [pltpu.make_async_copy(x_hbm.at[c], x_ref.at[c], x_sem.at[c]) for c in range(2)]
    for copy in loads:
        copy.start()

    i = iota((SIDE, SIDE), 0)
    raw = iota((SIDE, SIDE), 1)
    pair = ((i >> 4) == (raw >> 4)) & (((i >> 1) & 7) == (raw & 7))
    for half in range(2):
        pool_ref[half * SIDE : (half + 1) * SIDE, :] = jnp.where(
            pair & (((raw >> 3) & 1) == half), 0.25, 0.0
        ).astype(bf16)

    row8 = iota((8, SIDE), 0)
    lane8 = iota((8, SIDE), 1)
    at_left = (lane8 == SIDE - 1 - row8) & (row8 < 3)
    at_right = (lane8 == row8) & (row8 < 3)
    lane16 = iota((16, SIDE), 1)
    offset = 64 + iota((16, SIDE), 0) - lane_row((16, SIDE), 1) + 3
    head = lane_row((8, SIDE), 1)
    band = jnp.where(row8 < 4, 2 - row8 - head, SIDE + 3 + (row8 - 4) - head)
    band = jnp.where((row8 & 3) == 3, -1, band)

    def store_weights(c, rows, value):
        high = value.astype(bf16)
        rhs_ref[c, rows, :SIDE] = high
        rhs_ref[c, rows, SIDE:] = (value - high.astype(f32)).astype(bf16)

    for copy in loads[:4]:
        copy.wait()
    for c in range(2):
        borders = []
        for q in range(KERNEL):
            base = jnp.zeros((16, SIDE), f32)
            border = jnp.zeros((8, SIDE), f32)
            for p in range(KERNEL):
                weight = kernel_ref[c, p * KERNEL + q]
                base = jnp.where(offset == p, weight, base)
                border = jnp.where(band == p, weight, border)
            for k in range(8):
                value = base if k == 4 else pltpu.roll(base, (16 * (k - 4)) % SIDE, 1)
                if k == 0:
                    value = jnp.where(lane16 >= SIDE - 16, 0.0, value)
                if k == 7:
                    value = jnp.where(lane16 < 16, 0.0, value)
                at = q * SIDE + k * 16
                store_weights(c, slice(at, at + 16), value)
            borders.append(border)
        borders.append(jnp.zeros((SIDE - 8 * KERNEL, SIDE), f32))
        store_weights(c, slice(KERNEL * SIDE, DEPTH), jnp.concatenate(borders, axis=0))

    for copy in loads[4:]:
        copy.wait()
    sends = []
    for c in range(2):

        def prepare(f, c=c):
            x = x_ref[c, f]
            y = x.T.astype(f32)
            x = x.astype(f32)
            yt_ref[c, f, 8 : 8 + SIDE, :] = y
            strip_ref[c, f * 4] = x[:8]
            flip_ref[c, f * 4] = flip_head(x[:8])
            strip_ref[c, f * 4 + 1] = flip_tail(x[SIDE - 8 :])
            flip_ref[c, f * 4 + 1] = x[SIDE - 8 :]
            strip_ref[c, f * 4 + 2] = y[:8]
            flip_ref[c, f * 4 + 2] = flip_head(y[:8])
            strip_ref[c, f * 4 + 3] = flip_tail(y[SIDE - 8 :])
            flip_ref[c, f * 4 + 3] = y[SIDE - 8 :]

        for f in range(FACES):
            prepare(f)

        def assemble(f, c=c):
            at = [face_ref[s, f] * 4 + side_ref[s, f] for s in range(4)]
            left = strip_ref[c, at[2]]
            right = strip_ref[c, at[3]]
            yt_ref[c, f, :8, :] = flip_ref[c, at[2]]
            yt_ref[c, f, 8 + SIDE :, :] = right
            bands = jnp.where(
                row8 < 4, strip_ref[c, at[0]], pltpu.roll(strip_ref[c, at[1]], 4, 0)
            )
            upper = jnp.where(at_left, left[:, :1], 0.0) + jnp.where(at_right, right[:, :1], 0.0)
            lower = jnp.where(at_left, left[:, SIDE - 1 :], 0.0) + jnp.where(
                at_right, right[:, SIDE - 1 :], 0.0
            )
            upper = jnp.sum(upper, axis=0, keepdims=True)
            lower = jnp.sum(lower, axis=0, keepdims=True)
            corner = 0.5 * (
                jnp.where(lane8 >= SIDE // 2, bands[:, :1], bands[:, SIDE - 1 :])
                + jnp.where(row8 < 4, upper, lower)
            )
            shifted = []
            for q in range(KERNEL):
                s = 3 - q
                if s > 0:
                    shifted.append(pltpu.roll(jnp.where(lane8 >= SIDE - s, corner, bands), s, 1))
                elif s < 0:
                    shifted.append(pltpu.roll(jnp.where(lane8 < -s, corner, bands), SIDE + s, 1))
                else:
                    shifted.append(bands)
            shifted.append(jnp.zeros((SIDE - 8 * KERNEL, SIDE), f32))
            rows = slice(f * SIDE, (f + 1) * SIDE)
            lhs_ref[rows, KERNEL * SIDE :] = jnp.concatenate(shifted, axis=0).astype(bf16).T
            for q in range(KERNEL):
                lhs_ref[rows, q * SIDE : (q + 1) * SIDE] = yt_ref[
                    c, f, 5 + q : 5 + q + SIDE, :
                ].astype(bf16)

        for f in range(FACES):
            assemble(f)

        bias = bias_ref[c]
        for part in range(3):
            product = jnp.dot(
                lhs_ref[part * 512 : (part + 1) * 512, :],
                rhs_ref[c],
                preferred_element_type=f32,
            )
            conv = product[:, :SIDE] + product[:, SIDE:] + bias
            for g in range(4):
                f = part * 4 + g
                for t in range(16):
                    at = g * SIDE + t * 8
                    out_ref[t, f * 8 : (f + 1) * 8, :] = conv[at : at + 8]
        middle = slice(3 * SIDE, 4 * SIDE)
        pooled = jnp.dot(
            lhs_ref[: 6 * SIDE, middle], pool_ref[:SIDE, :], preferred_element_type=f32
        ) + jnp.dot(lhs_ref[6 * SIDE :, middle], pool_ref[SIDE:, :], preferred_element_type=f32)
        for f in range(6):
            for t in range(16):
                at = f * SIDE + t * 8
                out_ref[t, 96 + f * 8 : 96 + (f + 1) * 8, :] = pooled[at : at + 8]

        def pack(t, c=c):
            block = jnp.concatenate(
                [
                    out_ref[t, pl.ds(0, 48, stride=2), :],
                    out_ref[t, pl.ds(1, 48, stride=2), :],
                    out_ref[t, pl.ds(96, 24, stride=2), :] + out_ref[t, pl.ds(97, 24, stride=2), :],
                    jnp.zeros((8, SIDE), f32),
                ],
                axis=0,
            )
            block = block.astype(bf16).T
            for ty in range(8):
                msg_ref[ty, t, c * 16 : (c + 1) * 16, :] = block[ty * 16 : (ty + 1) * 16]

        for t in range(16):
            pack(t)
        sends.append(
            pltpu.make_async_copy(
                msg_ref.at[:, :, pl.ds(c * 16, 16)],
                msg_hbm.at[:, :, pl.ds(c * 16, 16)],
                msg_sem.at[c],
            )
        )
        sends[-1].start()
    for copy in sends:
        copy.wait()


def send(features, conv_kernel, conv_bias, neighbour_face, neighbour_side):
    hbm = pl.BlockSpec(memory_space=pl.ANY)
    return pl.pallas_call(
        send_kernel,
        out_shape=jax.ShapeDtypeStruct((8, 16, 32, SIDE), bf16),
        in_specs=[hbm] * 5,
        out_specs=hbm,
        scratch_shapes=[
            pltpu.SMEM((2, KERNEL * KERNEL), f32),
            pltpu.SMEM((4, FACES), jnp.int32),
            pltpu.SMEM((4, FACES), jnp.int32),
            pltpu.SMEM((2,), f32),
            pltpu.VMEM((2, FACES, SIDE, SIDE), bf16),
            pltpu.VMEM((2, FACES, PADDED, SIDE), f32),
            pltpu.VMEM((2, FACES * 4, 8, SIDE), f32),
            pltpu.VMEM((2, FACES * 4, 8, SIDE), f32),
            pltpu.VMEM((FACES * SIDE, DEPTH), bf16),
            pltpu.VMEM((2, DEPTH, 2 * SIDE), bf16),
            pltpu.VMEM((2 * SIDE, SIDE), bf16),
            pltpu.VMEM((16, 144, SIDE), f32),
            pltpu.VMEM((8, 16, 32, SIDE), bf16),
            pltpu.SemaphoreType.DMA((4,)),
            pltpu.SemaphoreType.DMA((2,)),
            pltpu.SemaphoreType.DMA((2,)),
        ],
        cost_estimate=pl.CostEstimate(
            flops=2 * 2 * 1536 * DEPTH * 256, bytes_accessed=4000000, transcendentals=0
        ),
        compiler_params=pltpu.CompilerParams(vmem_limit_bytes=VMEM_LIMIT),
    )(conv_kernel.T, neighbour_face.T, neighbour_side.T, conv_bias, features)


def receive_kernel(
    msg_ref,
    vector_ref,
    expand_ref,
    reduce_ref,
    project_ref,
    weight_hbm,
    state_hbm,
    held_hbm,
    out_hbm,
    input_ref,
    from_state_ref,
    hidden_ref,
    out_ref,
    wide_ref,
    normed_ref,
    pooled_ref,
    units_ref,
    sems,
    out_sem,
):
    operands = [
        (weight_hbm.at[pl.ds(0, 512)], input_ref),
        (state_hbm.at[pl.ds(0, 384)], from_state_ref),
        (held_hbm.at[pl.ds(0, FACES)], hidden_ref),
    ]
    loads = [
        pltpu.make_async_copy(source, target, sems.at[k])
        for k, (source, target) in enumerate(operands)
    ]
    for copy in loads:
        copy.start()

    def vector(k, lanes):
        return vector_ref[k : k + 1, lanes]

    def column(k):
        row = vector(k, slice(0, 256))
        halves = [row[:, :SIDE], row[:, SIDE:]]
        return jnp.concatenate([jnp.broadcast_to(v, (SIDE, SIDE)).T for v in halves], axis=0)

    gain = column(5)
    shift = column(6)
    wide_ref[...] = msg_ref[...].astype(f32)
    lane = iota((256, SIDE), 1)
    for r in range(16):
        di, ci = r // 8, r % 8
        values = wide_ref[pl.ds(r, 256, stride=16), :]
        center = jnp.sum(values, axis=0, keepdims=True) * (1.0 / 256)
        away = values - center
        spread = jnp.sum(away * away, axis=0, keepdims=True) * (1.0 / 256)
        normed = away * lax.rsqrt(spread + EPSILON) * gain + shift
        cells = jnp.where(lane < 96, normed, values).astype(bf16).T
        rows = slice(ci * 48, (ci + 1) * 48)
        normed_ref[di * 2, rows, :] = cells[:48]
        normed_ref[di * 2 + 1, rows, :] = cells[48:96]
        pooled_ref[ci * 48 + di * 24 : ci * 48 + (di + 1) * 24, :] = cells[96:].astype(f32)[:24]

    for k in range(4):
        lanes = slice(k * 256, (k + 1) * 256)
        for m in range(3):
            rows = slice(m * 128, (m + 1) * 128)
            hidden = jnp.dot(
                normed_ref[:, rows, :].reshape(512, 256),
                expand_ref[:, lanes],
                preferred_element_type=f32,
            )
            total = None
            for s in range(4):
                part = hidden[s * 128 : (s + 1) * 128] + vector(0, lanes)
                unit = part * (1.0 + lax.erf(part * (0.5**0.5)))
                total = unit if total is None else total + unit
            units_ref[rows, lanes] = total.astype(bf16)

    update = (
        jnp.dot(units_ref[...], reduce_ref[...], preferred_element_type=f32) * 0.125
        + vector(1, slice(0, 256))
    ) * vector(2, slice(0, 256))
    pooled = (pooled_ref[...] + update).astype(bf16)
    mapped = (
        jnp.dot(pooled, project_ref[...], preferred_element_type=f32) + vector(3, slice(0, 512))
    ).astype(bf16)

    for copy in loads:
        copy.wait()

    def sigmoid(v):
        return 0.5 * jnp.tanh(0.5 * v) + 0.5

    sends = []
    for k in range(2):

        def gate(block):
            lanes = slice(block * 512 + k * 256, block * 512 + (k + 1) * 256)
            return (
                jnp.dot(mapped, input_ref[:, lanes], preferred_element_type=f32)
                + vector(4, lanes),
                from_state_ref[:, lanes],
            )

        lanes = slice(k * 256, (k + 1) * 256)
        a, b = gate(0)
        update_gate = sigmoid(a + b)
        a, b = gate(1)
        reset_gate = sigmoid(a + b)
        a, b = gate(2)
        candidate = jnp.tanh(a + reset_gate * b)
        for ci in range(8):
            for f in range(FACES):
                rows = slice(ci * 48 + f * 4, ci * 48 + f * 4 + 4)
                kept = candidate[rows]
                out_ref[f, ci, :, lanes] = kept + update_gate[rows] * (
                    hidden_ref[f, ci, :, lanes] - kept
                )
        sends.append(
            pltpu.make_async_copy(
                out_ref.at[:, :, :, lanes], out_hbm.at[:, :, :, lanes], out_sem.at[k]
            )
        )
        sends[-1].start()
    for copy in sends:
        copy.wait()


def ready_kernel(
    hidden_hbm,
    state_hbm,
    state_bias_hbm,
    gain_hbm,
    shift_hbm,
    expand_bias_hbm,
    reduce_bias_hbm,
    scale_hbm,
    project_bias_hbm,
    input_bias_hbm,
    expand_hbm,
    reduce_hbm,
    project_hbm,
    input_hbm,
    vector_ref,
    expand_ref,
    reduce_ref,
    project_ref,
    weight_hbm,
    state_part_hbm,
    held_hbm,
    hidden_ref,
    state_ref,
    state_bias_ref,
    gain_ref,
    shift_ref,
    expand_bias_ref,
    reduce_bias_ref,
    scale_ref,
    project_bias_ref,
    input_bias_ref,
    previous_ref,
    from_state_ref,
    input_ref,
    sems,
    pack_sems,
):
    packs = [
        pltpu.make_async_copy(source, target, pack_sems.at[k])
        for k, (source, target) in enumerate(
            [
                (expand_hbm, expand_ref),
                (reduce_hbm, reduce_ref),
                (project_hbm, project_ref),
                (input_hbm, input_ref),
            ]
        )
    ]
    for copy in packs:
        copy.start()
    operands = [
        (hidden_hbm, hidden_ref),
        (state_hbm, state_ref),
        (state_bias_hbm, state_bias_ref),
        (gain_hbm, gain_ref),
        (shift_hbm, shift_ref),
        (expand_bias_hbm, expand_bias_ref),
        (reduce_bias_hbm, reduce_bias_ref),
        (scale_hbm, scale_ref),
        (project_bias_hbm, project_bias_ref),
        (input_bias_hbm, input_bias_ref),
    ]
    loads = [
        pltpu.make_async_copy(source, target, sems.at[k])
        for k, (source, target) in enumerate(operands)
    ]
    for copy in loads:
        copy.start()
    for copy in loads + packs:
        copy.wait()
    packs = [
        pltpu.make_async_copy(source, target, pack_sems.at[4 + k])
        for k, (source, target) in enumerate(
            [
                (input_ref, weight_hbm.at[pl.ds(0, 512)]),
                (hidden_ref, held_hbm.at[pl.ds(0, FACES)]),
            ]
        )
    ]
    for copy in packs:
        copy.start()
    for ci in range(8):
        for f in range(FACES):
            at = ci * 48 + f * 4
            previous_ref[at : at + 4, :] = hidden_ref[f, ci]
    for k in range(6):
        lanes = slice(k * 256, (k + 1) * 256)
        from_state_ref[:, lanes] = (
            jnp.dot(
                previous_ref[...].astype(bf16), state_ref[:, lanes], preferred_element_type=f32
            )
            + state_bias_ref[:, lanes]
        )
    packs.append(
        pltpu.make_async_copy(
            from_state_ref, state_part_hbm.at[pl.ds(0, 384)], pack_sems.at[6]
        )
    )
    packs[-1].start()
    vectors = (
        expand_bias_ref,
        reduce_bias_ref,
        scale_ref,
        project_bias_ref,
        input_bias_ref,
        gain_ref,
        shift_ref,
    )
    for k, source in enumerate(vectors):
        vector_ref[k : k + 1, : source.shape[1]] = source[...]
    for copy in packs:
        copy.wait()


def ready(hidden, state_gates, vectors, weights):
    vmem = pl.BlockSpec(memory_space=pltpu.VMEM)
    hbm = pl.BlockSpec(memory_space=pl.ANY)
    operands = (hidden, state_gates) + tuple(v.reshape(1, -1) for v in vectors)
    return pl.pallas_call(
        ready_kernel,
        out_shape=(
            jax.ShapeDtypeStruct((8, 1536), f32),
            *(jax.ShapeDtypeStruct(v.shape, v.dtype) for v in weights[:3]),
            jax.ShapeDtypeStruct((WEIGHT_ROWS, 1536), bf16),
            jax.ShapeDtypeStruct((STATE_ROWS, 1536), f32),
            jax.ShapeDtypeStruct((STATE_FACES, 8, 4, 512), f32),
        ),
        in_specs=[hbm] * (len(operands) + len(weights)),
        out_specs=(vmem,) * 4 + (hbm,) * 3,
        scratch_shapes=[pltpu.VMEM(v.shape, v.dtype) for v in operands]
        + [
            pltpu.VMEM((384, 512), f32),
            pltpu.VMEM((384, 1536), f32),
            pltpu.VMEM((512, 1536), bf16),
            pltpu.SemaphoreType.DMA((len(operands),)),
            pltpu.SemaphoreType.DMA((7,)),
        ],
        cost_estimate=pl.CostEstimate(
            flops=2 * 384 * 512 * 1536, bytes_accessed=8000000, transcendentals=0
        ),
        compiler_params=pltpu.CompilerParams(vmem_limit_bytes=READY_VMEM),
    )(*operands, *weights)


def receive(*operands):
    vmem = pl.BlockSpec(memory_space=pltpu.VMEM)
    hbm = pl.BlockSpec(memory_space=pl.ANY)
    result = jax.ShapeDtypeStruct((FACES, 8, 4, 512), f32)
    return pl.pallas_call(
        receive_kernel,
        out_shape=result,
        in_specs=[vmem] * 5 + [hbm] * 3,
        out_specs=hbm,
        scratch_shapes=[
            pltpu.VMEM((512, 1536), bf16),
            pltpu.VMEM((384, 1536), f32),
            pltpu.VMEM(result.shape, f32),
            pltpu.VMEM(result.shape, f32),
            pltpu.VMEM((4096, SIDE), f32),
            pltpu.VMEM((4, 384, 256), bf16),
            pltpu.VMEM((384, 256), f32),
            pltpu.VMEM((384, 1024), bf16),
            pltpu.SemaphoreType.DMA((3,)),
            pltpu.SemaphoreType.DMA((2,)),
        ],
        cost_estimate=pl.CostEstimate(
            flops=2 * 700000000, bytes_accessed=8000000, transcendentals=2000000
        ),
        compiler_params=pltpu.CompilerParams(vmem_limit_bytes=RECEIVE_VMEM),
    )(*operands)


def shards(
    features,
    conv_kernel,
    conv_bias,
    neighbour_face,
    neighbour_side,
    norm_gain,
    norm_shift,
    expand_weight,
    expand_bias,
    reduce_weight,
    reduce_bias,
    layer_scale,
    project_weight,
    project_bias,
    input_gates,
    input_bias,
    state_gates,
    state_bias,
    hidden_state,
):
    message = send(features, conv_kernel, conv_bias, neighbour_face, neighbour_side)
    message = message.reshape(128, 32, SIDE)
    arrived = lax.all_to_all(message, ("ty", "tx"), split_axis=0, concat_axis=0, tiled=True)
    operands = ready(
        hidden_state,
        state_gates,
        (
            state_bias,
            norm_gain,
            norm_shift,
            expand_bias,
            reduce_bias,
            layer_scale,
            project_bias,
            input_bias,
        ),
        (expand_weight, reduce_weight, project_weight, input_gates),
    )
    return receive(arrived.reshape(4096, SIDE), *operands)


def solution(mesh):
    placed = (
        P(("ty", "tx"), None, None, None),
        P(None, ("ty", "tx")),
        P(("ty", "tx")),
        P(),
        P(),
        P(),
        P(),
        P(),
        P(),
        P(),
        P(),
        P(),
        P(),
        P(),
        P(),
        P(),
        P(),
        P(),
        P(None, "ty", "tx", None),
    )
    return jax.shard_map(
        shards, mesh=mesh, in_specs=placed, out_specs=P(None, "ty", "tx", None), check_vma=False
    )
```

```python
import jax
import jax.numpy as jnp
from jax import lax
from jax.experimental import pallas as pl
from jax.experimental.pallas import tpu as pltpu
from jax.sharding import PartitionSpec as P

KERNEL = 7
FACES = 12
SIDE = 128
EPSILON = 1e-06
PADDED = SIDE + 16
DEPTH = (KERNEL + 1) * SIDE

VMEM_LIMIT = 63 * 1024 * 1024
READY_VMEM = 52 * 1024 * 1024
RECEIVE_VMEM = 44 * 1024 * 1024
WEIGHT_ROWS = 8192
STATE_FACES = 34 * FACES
STATE_ROWS = 4096

f32 = jnp.float32
bf16 = jnp.bfloat16


def iota(shape, axis):
    return lax.broadcasted_iota(jnp.int32, shape, axis)


def flip_head(tile):
    row = iota(tile.shape, 0)
    return jnp.where(
        row == 7,
        pltpu.roll(tile, 7, 0),
        jnp.where(row == 6, pltpu.roll(tile, 5, 0), pltpu.roll(tile, 3, 0)),
    )


def flip_tail(tile):
    row = iota(tile.shape, 0)
    return jnp.where(
        row == 0,
        pltpu.roll(tile, 1, 0),
        jnp.where(row == 1, pltpu.roll(tile, 3, 0), pltpu.roll(tile, 5, 0)),
    )


def lane_row(shape, axis):
    n = iota(shape, axis)
    return (n & ~15) + ((n & 7) << 1) + ((n >> 3) & 1)


def send_kernel(
    kernel_hbm,
    face_hbm,
    side_hbm,
    bias_hbm,
    x_hbm,
    msg_hbm,
    kernel_ref,
    face_ref,
    side_ref,
    bias_ref,
    x_ref,
    yt_ref,
    strip_ref,
    flip_ref,
    lhs_ref,
    rhs_ref,
    pool_ref,
    out_ref,
    msg_ref,
    small_sem,
    x_sem,
    msg_sem,
):
    loads = [
        pltpu.make_async_copy(source, target, small_sem.at[k])
        for k, (source, target) in enumerate(
            [
                (kernel_hbm, kernel_ref),
                (face_hbm, face_ref),
                (side_hbm, side_ref),
                (bias_hbm, bias_ref),
            ]
        )
    ] + [pltpu.make_async_copy(x_hbm.at[c], x_ref.at[c], x_sem.at[c]) for c in range(2)]
    for copy in loads[4:] + loads[:4]:
        copy.start()

    i = iota((SIDE, SIDE), 0)
    raw = iota((SIDE, SIDE), 1)
    pair = ((i >> 4) == (raw >> 4)) & (((i >> 1) & 7) == (raw & 7))
    for half in range(2):
        pool_ref[half * SIDE : (half + 1) * SIDE, :] = jnp.where(
            pair & (((raw >> 3) & 1) == half), 0.25, 0.0
        ).astype(bf16)

    row8 = iota((8, SIDE), 0)
    lane8 = iota((8, SIDE), 1)
    at_left = (lane8 == SIDE - 1 - row8) & (row8 < 3)
    at_right = (lane8 == row8) & (row8 < 3)
    lane16 = iota((16, SIDE), 1)
    offset = 64 + iota((16, SIDE), 0) - lane_row((16, SIDE), 1) + 3
    head = lane_row((8, SIDE), 1)
    band = jnp.where(row8 < 4, 2 - row8 - head, SIDE + 3 + (row8 - 4) - head)
    band = jnp.where((row8 & 3) == 3, -1, band)

    def store_weights(c, rows, value):
        high = value.astype(bf16)
        rhs_ref[c, rows, :SIDE] = high
        rhs_ref[c, rows, SIDE:] = (value - high.astype(f32)).astype(bf16)

    for copy in loads[:4]:
        copy.wait()
    for c in range(2):
        borders = []
        for q in range(KERNEL):
            base = jnp.zeros((16, SIDE), f32)
            border = jnp.zeros((8, SIDE), f32)
            for p in range(KERNEL):
                weight = kernel_ref[c, p * KERNEL + q]
                base = jnp.where(offset == p, weight, base)
                border = jnp.where(band == p, weight, border)
            for k in range(8):
                value = base if k == 4 else pltpu.roll(base, (16 * (k - 4)) % SIDE, 1)
                if k == 0:
                    value = jnp.where(lane16 >= SIDE - 16, 0.0, value)
                if k == 7:
                    value = jnp.where(lane16 < 16, 0.0, value)
                at = q * SIDE + k * 16
                store_weights(c, slice(at, at + 16), value)
            borders.append(border)
        borders.append(jnp.zeros((SIDE - 8 * KERNEL, SIDE), f32))
        store_weights(c, slice(KERNEL * SIDE, DEPTH), jnp.concatenate(borders, axis=0))

    for copy in loads[4:]:
        copy.wait()
    sends = []
    for c in range(2):

        def prepare(f, c=c):
            x = x_ref[c, f]
            y = x.T.astype(f32)
            x = x.astype(f32)
            yt_ref[c, f, 8 : 8 + SIDE, :] = y
            strip_ref[c, f * 4] = x[:8]
            flip_ref[c, f * 4] = flip_head(x[:8])
            strip_ref[c, f * 4 + 1] = flip_tail(x[SIDE - 8 :])
            flip_ref[c, f * 4 + 1] = x[SIDE - 8 :]
            strip_ref[c, f * 4 + 2] = y[:8]
            flip_ref[c, f * 4 + 2] = flip_head(y[:8])
            strip_ref[c, f * 4 + 3] = flip_tail(y[SIDE - 8 :])
            flip_ref[c, f * 4 + 3] = y[SIDE - 8 :]

        for f in range(FACES):
            prepare(f)

        def assemble(f, c=c):
            at = [face_ref[s, f] * 4 + side_ref[s, f] for s in range(4)]
            left = strip_ref[c, at[2]]
            right = strip_ref[c, at[3]]
            yt_ref[c, f, :8, :] = flip_ref[c, at[2]]
            yt_ref[c, f, 8 + SIDE :, :] = right
            bands = jnp.where(
                row8 < 4, strip_ref[c, at[0]], pltpu.roll(strip_ref[c, at[1]], 4, 0)
            )
            upper = jnp.where(at_left, left[:, :1], 0.0) + jnp.where(at_right, right[:, :1], 0.0)
            lower = jnp.where(at_left, left[:, SIDE - 1 :], 0.0) + jnp.where(
                at_right, right[:, SIDE - 1 :], 0.0
            )
            upper = jnp.sum(upper, axis=0, keepdims=True)
            lower = jnp.sum(lower, axis=0, keepdims=True)
            corner = 0.5 * (
                jnp.where(lane8 >= SIDE // 2, bands[:, :1], bands[:, SIDE - 1 :])
                + jnp.where(row8 < 4, upper, lower)
            )
            shifted = []
            for q in range(KERNEL):
                s = 3 - q
                if s > 0:
                    shifted.append(pltpu.roll(jnp.where(lane8 >= SIDE - s, corner, bands), s, 1))
                elif s < 0:
                    shifted.append(pltpu.roll(jnp.where(lane8 < -s, corner, bands), SIDE + s, 1))
                else:
                    shifted.append(bands)
            shifted.append(jnp.zeros((SIDE - 8 * KERNEL, SIDE), f32))
            rows = slice(f * SIDE, (f + 1) * SIDE)
            lhs_ref[rows, KERNEL * SIDE :] = jnp.concatenate(shifted, axis=0).astype(bf16).T
            for q in range(KERNEL):
                lhs_ref[rows, q * SIDE : (q + 1) * SIDE] = yt_ref[
                    c, f, 5 + q : 5 + q + SIDE, :
                ].astype(bf16)

        for f in range(FACES):
            assemble(f)

        bias = bias_ref[c]
        for part in range(3):
            product = jnp.dot(
                lhs_ref[part * 512 : (part + 1) * 512, :],
                rhs_ref[c],
                preferred_element_type=f32,
            )
            conv = product[:, :SIDE] + product[:, SIDE:] + bias
            for g in range(4):
                f = part * 4 + g
                for t in range(16):
                    at = g * SIDE + t * 8
                    out_ref[t, f * 8 : (f + 1) * 8, :] = conv[at : at + 8]
        middle = slice(3 * SIDE, 4 * SIDE)
        pooled = jnp.dot(
            lhs_ref[: 6 * SIDE, middle], pool_ref[:SIDE, :], preferred_element_type=f32
        ) + jnp.dot(lhs_ref[6 * SIDE :, middle], pool_ref[SIDE:, :], preferred_element_type=f32)
        for f in range(6):
            for t in range(16):
                at = f * SIDE + t * 8
                out_ref[t, 96 + f * 8 : 96 + (f + 1) * 8, :] = pooled[at : at + 8]

        def pack(t, c=c):
            block = jnp.concatenate(
                [
                    out_ref[t, pl.ds(0, 48, stride=2), :],
                    out_ref[t, pl.ds(1, 48, stride=2), :],
                    out_ref[t, pl.ds(96, 24, stride=2), :] + out_ref[t, pl.ds(97, 24, stride=2), :],
                    jnp.zeros((8, SIDE), f32),
                ],
                axis=0,
            )
            block = block.astype(bf16).T
            for ty in range(8):
                msg_ref[ty, t, c * 16 : (c + 1) * 16, :] = block[ty * 16 : (ty + 1) * 16]

        for t in range(16):
            pack(t)
        sends.append(
            pltpu.make_async_copy(
                msg_ref.at[:, :, pl.ds(c * 16, 16)],
                msg_hbm.at[:, :, pl.ds(c * 16, 16)],
                msg_sem.at[c],
            )
        )
        sends[-1].start()
    for copy in sends:
        copy.wait()


def send(features, conv_kernel, conv_bias, neighbour_face, neighbour_side):
    hbm = pl.BlockSpec(memory_space=pl.ANY)
    return pl.pallas_call(
        send_kernel,
        out_shape=jax.ShapeDtypeStruct((8, 16, 32, SIDE), bf16),
        in_specs=[hbm] * 5,
        out_specs=hbm,
        scratch_shapes=[
            pltpu.SMEM((2, KERNEL * KERNEL), f32),
            pltpu.SMEM((4, FACES), jnp.int32),
            pltpu.SMEM((4, FACES), jnp.int32),
            pltpu.SMEM((2,), f32),
            pltpu.VMEM((2, FACES, SIDE, SIDE), bf16),
            pltpu.VMEM((2, FACES, PADDED, SIDE), f32),
            pltpu.VMEM((2, FACES * 4, 8, SIDE), f32),
            pltpu.VMEM((2, FACES * 4, 8, SIDE), f32),
            pltpu.VMEM((FACES * SIDE, DEPTH), bf16),
            pltpu.VMEM((2, DEPTH, 2 * SIDE), bf16),
            pltpu.VMEM((2 * SIDE, SIDE), bf16),
            pltpu.VMEM((16, 144, SIDE), f32),
            pltpu.VMEM((8, 16, 32, SIDE), bf16),
            pltpu.SemaphoreType.DMA((4,)),
            pltpu.SemaphoreType.DMA((2,)),
            pltpu.SemaphoreType.DMA((2,)),
        ],
        cost_estimate=pl.CostEstimate(
            flops=2 * 2 * 1536 * DEPTH * 256, bytes_accessed=4000000, transcendentals=0
        ),
        compiler_params=pltpu.CompilerParams(vmem_limit_bytes=VMEM_LIMIT),
    )(conv_kernel.T, neighbour_face.T, neighbour_side.T, conv_bias, features)


def receive_kernel(
    msg_ref,
    vector_ref,
    expand_ref,
    reduce_ref,
    project_ref,
    weight_hbm,
    state_hbm,
    held_hbm,
    out_hbm,
    input_ref,
    from_state_ref,
    hidden_ref,
    out_ref,
    wide_ref,
    normed_ref,
    pooled_ref,
    units_ref,
    sems,
    out_sem,
):
    operands = [
        (weight_hbm.at[pl.ds(0, 512)], input_ref),
        (state_hbm.at[pl.ds(0, 384)], from_state_ref),
        (held_hbm.at[pl.ds(0, FACES)], hidden_ref),
    ]
    loads = [
        pltpu.make_async_copy(source, target, sems.at[k])
        for k, (source, target) in enumerate(operands)
    ]
    for copy in loads:
        copy.start()

    def vector(k, lanes):
        return vector_ref[k : k + 1, lanes]

    def column(k):
        row = vector(k, slice(0, 256))
        halves = [row[:, :SIDE], row[:, SIDE:]]
        return jnp.concatenate([jnp.broadcast_to(v, (SIDE, SIDE)).T for v in halves], axis=0)

    gain = column(5)
    shift = column(6)
    wide_ref[...] = msg_ref[...].astype(f32)
    lane = iota((256, SIDE), 1)
    for r in range(16):
        di, ci = r // 8, r % 8
        values = wide_ref[pl.ds(r, 256, stride=16), :]
        center = jnp.sum(values, axis=0, keepdims=True) * (1.0 / 256)
        away = values - center
        spread = jnp.sum(away * away, axis=0, keepdims=True) * (1.0 / 256)
        normed = away * lax.rsqrt(spread + EPSILON) * gain + shift
        cells = jnp.where(lane < 96, normed, values).astype(bf16).T
        rows = slice(ci * 48, (ci + 1) * 48)
        normed_ref[di * 2, rows, :] = cells[:48]
        normed_ref[di * 2 + 1, rows, :] = cells[48:96]
        pooled_ref[ci * 48 + di * 24 : ci * 48 + (di + 1) * 24, :] = cells[96:].astype(f32)[:24]

    for k in range(4):
        lanes = slice(k * 256, (k + 1) * 256)
        for m in range(3):
            rows = slice(m * 128, (m + 1) * 128)
            hidden = jnp.dot(
                normed_ref[:, rows, :].reshape(512, 256),
                expand_ref[:, lanes],
                preferred_element_type=f32,
            )
            total = None
            for s in range(4):
                part = hidden[s * 128 : (s + 1) * 128] + vector(0, lanes)
                unit = part + part * lax.erf(part * (0.5**0.5))
                total = unit if total is None else total + unit
            units_ref[rows, lanes] = total.astype(bf16)

    update = (
        jnp.dot(units_ref[...], reduce_ref[...], preferred_element_type=f32) * 0.125
        + vector(1, slice(0, 256))
    ) * vector(2, slice(0, 256))
    pooled = (pooled_ref[...] + update).astype(bf16)
    mapped = (
        jnp.dot(pooled, project_ref[...], preferred_element_type=f32) + vector(3, slice(0, 512))
    ).astype(bf16)

    for copy in loads:
        copy.wait()

    def sigmoid(v):
        return 0.5 * jnp.tanh(0.5 * v) + 0.5

    sends = []
    for k in range(2):

        def gate(block):
            lanes = slice(block * 512 + k * 256, block * 512 + (k + 1) * 256)
            return (
                jnp.dot(mapped, input_ref[:, lanes], preferred_element_type=f32)
                + vector(4, lanes),
                from_state_ref[:, lanes],
            )

        lanes = slice(k * 256, (k + 1) * 256)
        a, b = gate(0)
        update_gate = sigmoid(a + b)
        a, b = gate(1)
        reset_gate = sigmoid(a + b)
        a, b = gate(2)
        candidate = jnp.tanh(a + reset_gate * b)
        for ci in range(8):
            for f in range(FACES):
                rows = slice(ci * 48 + f * 4, ci * 48 + f * 4 + 4)
                kept = candidate[rows]
                out_ref[f, ci, :, lanes] = kept + update_gate[rows] * (
                    hidden_ref[f, ci, :, lanes] - kept
                )
        sends.append(
            pltpu.make_async_copy(
                out_ref.at[:, :, :, lanes], out_hbm.at[:, :, :, lanes], out_sem.at[k]
            )
        )
        sends[-1].start()
    for copy in sends:
        copy.wait()


def ready_kernel(
    hidden_hbm,
    state_hbm,
    state_bias_hbm,
    gain_hbm,
    shift_hbm,
    expand_bias_hbm,
    reduce_bias_hbm,
    scale_hbm,
    project_bias_hbm,
    input_bias_hbm,
    expand_hbm,
    reduce_hbm,
    project_hbm,
    input_hbm,
    vector_ref,
    expand_ref,
    reduce_ref,
    project_ref,
    weight_hbm,
    state_part_hbm,
    held_hbm,
    hidden_ref,
    state_ref,
    state_bias_ref,
    gain_ref,
    shift_ref,
    expand_bias_ref,
    reduce_bias_ref,
    scale_ref,
    project_bias_ref,
    input_bias_ref,
    previous_ref,
    from_state_ref,
    input_ref,
    sems,
    pack_sems,
):
    packs = [
        pltpu.make_async_copy(source, target, pack_sems.at[k])
        for k, (source, target) in enumerate(
            [
                (expand_hbm, expand_ref),
                (reduce_hbm, reduce_ref),
                (project_hbm, project_ref),
                (input_hbm, input_ref),
            ]
        )
    ]
    for copy in packs:
        copy.start()
    operands = [
        (hidden_hbm, hidden_ref),
        (state_hbm, state_ref),
        (state_bias_hbm, state_bias_ref),
        (gain_hbm, gain_ref),
        (shift_hbm, shift_ref),
        (expand_bias_hbm, expand_bias_ref),
        (reduce_bias_hbm, reduce_bias_ref),
        (scale_hbm, scale_ref),
        (project_bias_hbm, project_bias_ref),
        (input_bias_hbm, input_bias_ref),
    ]
    loads = [
        pltpu.make_async_copy(source, target, sems.at[k])
        for k, (source, target) in enumerate(operands)
    ]
    for copy in loads:
        copy.start()
    for copy in loads + packs:
        copy.wait()
    packs = [
        pltpu.make_async_copy(source, target, pack_sems.at[4 + k])
        for k, (source, target) in enumerate(
            [
                (input_ref, weight_hbm.at[pl.ds(0, 512)]),
                (hidden_ref, held_hbm.at[pl.ds(0, FACES)]),
            ]
        )
    ]
    for copy in packs:
        copy.start()
    for ci in range(8):
        for f in range(FACES):
            at = ci * 48 + f * 4
            previous_ref[at : at + 4, :] = hidden_ref[f, ci]
    for k in range(6):
        lanes = slice(k * 256, (k + 1) * 256)
        from_state_ref[:, lanes] = (
            jnp.dot(
                previous_ref[...].astype(bf16), state_ref[:, lanes], preferred_element_type=f32
            )
            + state_bias_ref[:, lanes]
        )
    packs.append(
        pltpu.make_async_copy(
            from_state_ref, state_part_hbm.at[pl.ds(0, 384)], pack_sems.at[6]
        )
    )
    packs[-1].start()
    vectors = (
        expand_bias_ref,
        reduce_bias_ref,
        scale_ref,
        project_bias_ref,
        input_bias_ref,
        gain_ref,
        shift_ref,
    )
    for k, source in enumerate(vectors):
        vector_ref[k : k + 1, : source.shape[1]] = source[...]
    for copy in packs:
        copy.wait()


def ready(hidden, state_gates, vectors, weights):
    vmem = pl.BlockSpec(memory_space=pltpu.VMEM)
    hbm = pl.BlockSpec(memory_space=pl.ANY)
    operands = (hidden, state_gates) + tuple(v.reshape(1, -1) for v in vectors)
    return pl.pallas_call(
        ready_kernel,
        out_shape=(
            jax.ShapeDtypeStruct((8, 1536), f32),
            *(jax.ShapeDtypeStruct(v.shape, v.dtype) for v in weights[:3]),
            jax.ShapeDtypeStruct((WEIGHT_ROWS, 1536), bf16),
            jax.ShapeDtypeStruct((STATE_ROWS, 1536), f32),
            jax.ShapeDtypeStruct((STATE_FACES, 8, 4, 512), f32),
        ),
        in_specs=[hbm] * (len(operands) + len(weights)),
        out_specs=(vmem,) * 4 + (hbm,) * 3,
        scratch_shapes=[pltpu.VMEM(v.shape, v.dtype) for v in operands]
        + [
            pltpu.VMEM((384, 512), f32),
            pltpu.VMEM((384, 1536), f32),
            pltpu.VMEM((512, 1536), bf16),
            pltpu.SemaphoreType.DMA((len(operands),)),
            pltpu.SemaphoreType.DMA((7,)),
        ],
        cost_estimate=pl.CostEstimate(
            flops=2 * 384 * 512 * 1536, bytes_accessed=8000000, transcendentals=0
        ),
        compiler_params=pltpu.CompilerParams(vmem_limit_bytes=READY_VMEM),
    )(*operands, *weights)


def receive(*operands):
    vmem = pl.BlockSpec(memory_space=pltpu.VMEM)
    hbm = pl.BlockSpec(memory_space=pl.ANY)
    result = jax.ShapeDtypeStruct((FACES, 8, 4, 512), f32)
    return pl.pallas_call(
        receive_kernel,
        out_shape=result,
        in_specs=[vmem] * 5 + [hbm] * 3,
        out_specs=hbm,
        scratch_shapes=[
            pltpu.VMEM((512, 1536), bf16),
            pltpu.VMEM((384, 1536), f32),
            pltpu.VMEM(result.shape, f32),
            pltpu.VMEM(result.shape, f32),
            pltpu.VMEM((4096, SIDE), f32),
            pltpu.VMEM((4, 384, 256), bf16),
            pltpu.VMEM((384, 256), f32),
            pltpu.VMEM((384, 1024), bf16),
            pltpu.SemaphoreType.DMA((3,)),
            pltpu.SemaphoreType.DMA((2,)),
        ],
        cost_estimate=pl.CostEstimate(
            flops=2 * 700000000, bytes_accessed=8000000, transcendentals=2000000
        ),
        compiler_params=pltpu.CompilerParams(vmem_limit_bytes=RECEIVE_VMEM),
    )(*operands)


def shards(
    features,
    conv_kernel,
    conv_bias,
    neighbour_face,
    neighbour_side,
    norm_gain,
    norm_shift,
    expand_weight,
    expand_bias,
    reduce_weight,
    reduce_bias,
    layer_scale,
    project_weight,
    project_bias,
    input_gates,
    input_bias,
    state_gates,
    state_bias,
    hidden_state,
):
    message = send(features, conv_kernel, conv_bias, neighbour_face, neighbour_side)
    message = message.reshape(128, 32, SIDE)
    arrived = lax.all_to_all(message, ("ty", "tx"), split_axis=0, concat_axis=0, tiled=True)
    operands = ready(
        hidden_state,
        state_gates,
        (
            state_bias,
            norm_gain,
            norm_shift,
            expand_bias,
            reduce_bias,
            layer_scale,
            project_bias,
            input_bias,
        ),
        (expand_weight, reduce_weight, project_weight, input_gates),
    )
    return receive(arrived.reshape(4096, SIDE), *operands)


def solution(mesh):
    placed = (
        P(("ty", "tx"), None, None, None),
        P(None, ("ty", "tx")),
        P(("ty", "tx")),
        P(),
        P(),
        P(),
        P(),
        P(),
        P(),
        P(),
        P(),
        P(),
        P(),
        P(),
        P(),
        P(),
        P(),
        P(),
        P(None, "ty", "tx", None),
    )
    return jax.shard_map(
        shards, mesh=mesh, in_specs=placed, out_specs=P(None, "ty", "tx", None), check_vma=False
    )
```
